32 devices in a mesh: groups: 2 (over y), wide: 4 (over z), tail: 2 (over x), sub: 2 (over core).
Axes of the slice: x: 2, y: 2, z: 4, core: 2. Of those that a mesh axis runs over, the one named last changes fastest.
Arguments:
- head_embed: float32 [512, 512], P(('groups', 'wide')), parts along dimension 0, may hold values from -2.1 to 2.1
- tail_embed: float32 [512, 512], P(('groups', 'tail'), 'sub'), parts along dimension 0, may hold values from -2.1 to 2.1
- core_mats: float32 [8, 512, 512], P(('groups', 'wide'), None, 'sub'), parts along dimension 0, may hold values from -0.25 to 0.25
- labels: int32 [512, 8, 256], P(('groups', 'wide'), None, 'tail'), parts along dimension 0, may hold values 0 or 1
- core_lists: int32 [4, 8], P(('groups', 'tail')), parts along dimension 0, may hold values from 0 to 3, as said below
Outputs:
- grad_head: float32 [512, 512], P(('groups', 'wide', 'tail', 'sub')), parts along dimension 0
- grad_tail: float32 [4, 128, 512], P(('groups', 'tail'), 'wide', 'sub'), parts along dimension 0
- grad_cores: float32 [8, 512, 512], P(('groups', 'tail'), 'wide', 'sub'), parts along dimension 0
The draws below stay inside these ranges and needn't reach their ends.
There are 2 independent parts, one for each index of `groups`. The reference program is written for one: setup_inputs(seed, part) draws one part's arguments, and reference() takes and returns one part's arrays. A program takes and returns all parts, laid end to end along the dimension named above; each array names one. Nothing has to cross between parts.
Inputs may be any that keep to these rules, and one draw needn't show every extreme that they name: `core_lists`: every one of the 4 core ids stands somewhere in the lists; ids may repeat.
All inputs are finite; a program needn't handle non-finite values. No bound on the sum of `labels` on one device may be relied on, other than what follows from the above.
Results may differ from the reference program's by a relative error of at most 0.0001.
Values sent between devices are 32-bit elements; how exact they have to be, the bound alone decides.
No kernel may reach another device: no remote copies, remote signals or barrier semaphores. Data moves between devices by JAX's collectives and lax.ppermute only.
A program may use at most 64 MiB of HBM per device.

```python
import math
import jax
import jax.numpy as jnp
from jax import lax

D = 512
LIST = 8
T_DEV = 128
NREL = 4
HEADS = 256
TAILS = 256
COLUMNS = 2


def draw_core_lists(key, part):
    first_key, second_key, third_key = jax.random.split(key, 3)
    covering = jax.random.permutation(first_key, NREL).astype(jnp.int32)
    remainder = jax.random.randint(second_key, (COLUMNS * LIST - NREL,), 0, NREL).astype(jnp.int32)
    flattened = jnp.concatenate([covering, remainder])
    shuffle_order = jax.random.permutation(third_key, COLUMNS * LIST)
    return flattened[shuffle_order].reshape(COLUMNS, LIST)


def set_ends(values, key, least, high):
    index_at = [jax.random.randint(jax.random.fold_in(key, axis), (), 0, length) for axis, length in enumerate(values.shape)]
    main_axis = values.shape.index(max(values.shape))
    beside = index_at[:main_axis] + [(index_at[main_axis] + 1) % values.shape[main_axis]] + index_at[main_axis + 1:]
    return values.at[tuple(index_at)].set(least).at[tuple(beside)].set(high)


def levels(rng, dims, cuts, least, top_value):
    gain, own = 1.0, jax.random.fold_in(rng, 6)
    for dim, parts in cuts:
        draws = jnp.exp(jax.random.uniform(jax.random.fold_in(own, dim), (parts,), jnp.float32, least / len(cuts), top_value / len(cuts)))
        gain = gain * jnp.repeat(draws, dims[dim] // parts).reshape([-1 if axis == dim else 1 for axis in range(len(dims))])
    return gain


def centred(own_key, extent, width, reach, shards=(), dtype=jnp.bfloat16):
    entries = jax.random.normal(own_key, extent, jnp.float32) * width
    if len(shards) > 0:
        entries = levels(own_key, extent, shards, -0.22, 0.18) * entries
    return jnp.clip(entries, min=-reach, max=reach).astype(dtype)


def setup_inputs(seed: int = 0, part: int = 0) -> dict:
    key_of = jax.random.split(jax.random.key(seed), 6)
    part_keys = jax.random.split(jax.random.fold_in(key_of[5], part), 6)
    return {
        "head_embed": centred(part_keys[0], (HEADS, D), 0.35, 2.1, ((0, 4),), jnp.float32),
        "tail_embed": centred(part_keys[1], (TAILS, D), 0.35, 2.1, ((0, 2), (1, 2)), jnp.float32),
        "core_mats": centred(part_keys[2], (NREL, D, D), D ** -0.5, 0.25, ((0, 4), (2, 2)), jnp.float32),
        "labels": set_ends((jax.random.randint(part_keys[3], (HEADS, LIST, TAILS), 0, 2) < 1).astype(jnp.int32), jax.random.fold_in(part_keys[3], 1), 0, 1),
        "core_lists": draw_core_lists(jax.random.fold_in(jax.random.fold_in(key_of[5], part), 71), part),
    }


def reference(head_embed, tail_embed, core_mats, labels, core_lists):
    highest = lax.Precision.HIGHEST
    grad_head = jnp.zeros((HEADS, D), jnp.float32)
    grad_cores = jnp.zeros((NREL, D, D), jnp.float32)
    tail_blocks = []
    for column in range(COLUMNS):
        tail_tile = tail_embed[column * T_DEV:(column + 1) * T_DEV]
        tail_total = jnp.zeros((T_DEV, D), jnp.float32)
        for slot_index in range(LIST):
            relation = core_lists[column, slot_index].astype(jnp.int32)
            matrix = lax.dynamic_index_in_dim(core_mats, relation, 0, keepdims=False)
            projected = jnp.dot(head_embed, matrix, precision=highest, preferred_element_type=jnp.float32)
            score_tile = jnp.dot(projected, tail_tile.T, precision=highest, preferred_element_type=jnp.float32)
            label_tile = labels[:, slot_index, column * T_DEV:(column + 1) * T_DEV].astype(jnp.float32)
            residual = jax.nn.sigmoid(score_tile) - label_tile
            weighted = jnp.dot(residual, tail_tile, precision=highest, preferred_element_type=jnp.float32)
            grad_head = grad_head + jnp.dot(weighted, matrix.T, precision=highest, preferred_element_type=jnp.float32)
            tail_total = tail_total + jnp.dot(residual.T, projected, precision=highest, preferred_element_type=jnp.float32)
            core_term = jnp.dot(head_embed.T, weighted, precision=highest, preferred_element_type=jnp.float32)
            grad_cores = grad_cores.at[relation].add(core_term)
        tail_blocks.append(tail_total)
    grad_tail = jnp.stack(tail_blocks)
    return (grad_head * (1.0 / math.sqrt(LIST * TAILS)), grad_tail * (1.0 / math.sqrt(LIST * HEADS)), grad_cores * (1.0 / math.sqrt(HEADS * T_DEV)))
```

```python
import functools
import math

import jax
import jax.numpy as jnp
from jax import lax
from jax.experimental import pallas as pl
from jax.experimental.pallas import tpu as pltpu
from jax.sharding import PartitionSpec as P


F32 = jnp.float32
VMEM_LIMIT = 48 * 1024 * 1024
NN = (((1,), (0,)), ((), ()))
NT = (((1,), (1,)), ((), ()))
TN = (((0,), (0,)), ((), ()))


def split(value):
    high = value.astype(jnp.bfloat16)
    low = (value - high.astype(F32)).astype(jnp.bfloat16)
    return high, low


def dot3(left, right, dims):
    lh, ll = left
    rh, rl = right
    mul = functools.partial(lax.dot_general, dimension_numbers=dims, preferred_element_type=F32)
    return mul(lh, rh) + (mul(lh, rl) + mul(ll, rh))


def rows_at(ref, index, count):
    if count % 8 == 0:
        return ref[pl.ds(pl.multiple_of(index * count, count), count), :]
    per = 8 // count
    window = ref[pl.ds(pl.multiple_of(index // per * 8, 8), 8), :]
    found = window[0:count]
    for i in range(1, per):
        found = jnp.where(index % per == i, window[i * count : (i + 1) * count], found)
    return found


def place():
    return lax.axis_index("wide"), lax.axis_index("tail"), lax.axis_index("sub")


def pack_kernel(wide, cols, list_ref, label_ref, head_ref, tail_ref, *outs):
    z_refs, x_ref, head_own, label_own = outs[: wide - 1], outs[-3], outs[-2], outs[-1]
    w, t, s = place()
    block, slots, width = label_ref.shape
    chunk = block // (2 * cols)
    rows = block // 2
    half = tail_ref.shape[1]
    for part in range(2):
        for col in range(cols):
            start = pl.multiple_of((col * 2 + (s ^ part)) * chunk, chunk)
            at = part * rows + col * chunk
            embed = head_ref[pl.ds(start, chunk), :]
            head_own[at : at + chunk, :] = embed
            slot_labels = [label_ref[pl.ds(start, chunk), j, :] for j in range(slots)]
            for k in range(wide):
                total = jnp.zeros((chunk, width), jnp.int32)
                for j in range(slots):
                    total = total + jnp.where(list_ref[0, j] == (w ^ k), slot_labels[j], 0)
                total = total.astype(F32)
                if k == 0:
                    label_own[at : at + chunk, :] = total
                    lane = (at // rows) * width
                    row = tail_ref.shape[0] + at % rows
                    x_ref[row : row + chunk, lane : lane + width] = total
                else:
                    z_refs[k - 1][at : at + chunk, half : half + width] = total
                    if part == 0:
                        z_refs[k - 1][at : at + chunk, 0:half] = embed[:, 0:half]
                        z_refs[k - 1][rows + at : rows + at + chunk, 0:half] = embed[:, half:]
    x_ref[0 : tail_ref.shape[0], :] = tail_ref[...]
    count = jnp.int32(0)
    for j in range(slots):
        count = count + (list_ref[0, j] == w).astype(jnp.int32)
    x_ref[tail_ref.shape[0] + rows :, :] = jnp.full((8, half), count.astype(F32), F32)


def query_kernel(core_ref, tail_ref, *refs):
    x_refs, out_ref = refs[:-1], refs[-1]
    depth = tail_ref.shape[0]
    tails = [tail_ref[...]] + [x[0:depth, :] for x in x_refs]
    out_ref[...] = dot3(split(core_ref[0]), split(jnp.concatenate(tails, axis=0)), NT)


def grad_kernel(wide, cols, refs):
    (list_ref, core_ref, query_ref, query_other, head_own, label_own, x_refs, z_refs, swap_refs, outs, own_ref,
     heads, resid, outer, tails) = refs
    w, t, s = place()
    block, dim = head_own.shape
    width = label_own.shape[1]
    rows = block // 2
    chunk = rows // cols
    half = core_ref.shape[2]
    heads[0:block, :] = head_own[...]
    for k in range(1, wide):
        at = k * block
        for part, ref in enumerate((z_refs[k - 1][0], swap_refs[k - 1][0])):
            heads[at + part * rows : at + part * rows + rows, 0:half] = ref[0:rows, 0:half]
            heads[at + part * rows : at + part * rows + rows, half:] = ref[rows:, 0:half]
    query = split(query_ref[...] + query_other[...])
    head_parts = split(heads[...])
    score = dot3(head_parts, query, NN)
    prob = jax.nn.sigmoid(score)
    count = jnp.int32(0)
    for j in range(list_ref.shape[1]):
        count = count + (list_ref[0, j] == w).astype(jnp.int32)
    depth = x_refs[0].shape[0] - 8 - rows if x_refs else 0
    for o in range(cols):
        lanes = slice(o * width, (o + 1) * width)
        times = count.astype(F32) if o == 0 else x_refs[o - 1][depth + rows : depth + rows + 1, 0:width]
        if o == 0:
            resid[0:block, lanes] = times * prob[0:block, lanes] - label_own[...]
        else:
            ref = x_refs[o - 1]
            for part in range(2):
                resid[part * rows : part * rows + rows, lanes] = (
                    times * prob[part * rows : part * rows + rows, lanes]
                    - ref[depth : depth + rows, part * width : (part + 1) * width]
                )
        for k in range(1, wide):
            first, last = (half, half + width) if o < 2 else (0, width)
            mine = z_refs[k - 1][o // 2][:, first:last]
            other = swap_refs[k - 1][o // 2]
            other = jnp.concatenate([other[rows:, first:last], other[0:rows, first:last]], axis=0)
            label = jnp.where(s == o % 2, mine, other)
            resid[k * block : (k + 1) * block, lanes] = times * prob[k * block : (k + 1) * block, lanes] - label
    resid_parts = split(resid[...])
    outer[...] = dot3(head_parts, resid_parts, TN)
    tails[...] = dot3(split(outer[:, 0:width]), split(core_ref[0]), TN)
    picked = [resid[pl.ds(pl.multiple_of(k * block + t * chunk, chunk), chunk), :] for k in range(wide)]
    head_sum = dot3(split(jnp.concatenate(picked, axis=0)), query, NT)
    core_rows = dim // wide
    tail_rows = width // wide
    span = core_rows // 2
    chunks = cols * width // half
    for k in range(wide):
        ref = own_ref if k == 0 else outs[k - 1]
        take = core_rows if k == 0 else span
        start = (w ^ k) * core_rows if k == 0 else (w ^ k) * core_rows + s * span
        piece = outer[pl.ds(pl.multiple_of(start, take), take), :]
        at = 0
        for i in range(chunks):
            ref[at : at + take, :] = piece[:, i * half : (i + 1) * half]
            at += take
        for i in range(dim // half):
            ref[at : at + chunk, :] = head_sum[k * chunk : (k + 1) * chunk, i * half : (i + 1) * half]
            at += chunk
        ref[at : at + tail_rows, :] = rows_at(tails, w ^ k, tail_rows)


def finish_kernel(wide, cols, scales, tail_ref, x_refs, own_ref, z_refs, swap_refs, head_out, tail_out, core_out, pieces):
    w, t, s = place()
    depth, half = tail_ref.shape
    core_rows = core_out.shape[1]
    span = core_rows // 2
    chunk, dim = head_out.shape
    tail_rows = tail_out.shape[1]
    chunks = cols * depth // half
    each = wide // cols
    for k in range(wide):
        relation = w ^ k

        @pl.when(relation // each == t)
        def _(k=k, at=relation % each):
            for i in range(chunks):
                lanes = slice(i * half, (i + 1) * half)
                if k == 0:
                    pieces[at, :, lanes] = own_ref[i * core_rows : (i + 1) * core_rows, :]
                else:
                    pieces[at, pl.ds(pl.multiple_of(s * span, span), span), lanes] = (
                        z_refs[k - 1][i * span : (i + 1) * span, :]
                    )
                    pieces[at, pl.ds(pl.multiple_of((1 - s) * span, span), span), lanes] = (
                        swap_refs[k - 1][i * span : (i + 1) * span, :]
                    )

    tails = split(jnp.concatenate([tail_ref[...]] + [x[0:depth, :] for x in x_refs], axis=0))
    for i in range(each):
        core_out[i] = dot3(split(pieces[i]), tails, NN) * scales[2]
    for i in range(dim // half):
        at = chunks * core_rows + i * chunk
        total = own_ref[at : at + chunk, :]
        for ref in z_refs:
            at = chunks * span + i * chunk
            total = total + ref[at : at + chunk, :]
        head_out[:, i * half : (i + 1) * half] = total * scales[0]
    at = chunks * core_rows + dim // half * chunk
    total = own_ref[at : at + tail_rows, :]
    for ref in z_refs:
        at = chunks * span + dim // half * chunk
        total = total + ref[at : at + tail_rows, :]
    tail_out[0] = total * scales[1]


def call(kernel, inputs, outputs, scratch=(), scalars=0, flops=0):
    vmem, smem = pl.BlockSpec(memory_space=pltpu.VMEM), pl.BlockSpec(memory_space=pltpu.SMEM)
    return pl.pallas_call(
        kernel,
        out_shape=tuple(jax.ShapeDtypeStruct(shape, F32) for shape in outputs),
        in_specs=[smem] * scalars + [vmem] * (len(inputs) - scalars),
        out_specs=tuple(vmem for _ in outputs),
        scratch_shapes=[pltpu.VMEM(shape, F32) for shape in scratch],
        compiler_params=pltpu.CompilerParams(vmem_limit_bytes=VMEM_LIMIT),
        cost_estimate=pl.CostEstimate(flops=flops, bytes_accessed=4 * sum(x.size for x in inputs), transcendentals=0),
    )(*inputs)


def body(head_embed, tail_embed, core_mats, labels, core_lists):
    wide, cols = lax.axis_size("wide"), lax.axis_size("tail")
    block, dim = head_embed.shape
    depth, half = tail_embed.shape
    slots = core_lists.shape[1]
    rows = block // 2
    chunk = rows // cols
    axes = ("wide", "tail", "sub")

    def move(value, k, offsets=(0, 0), flip=0):
        pairs = []
        for w in range(wide):
            for t in range(cols):
                for s in range(2):
                    target = ((w ^ k) * cols + (t ^ offsets[s])) * 2 + (s ^ flip)
                    pairs.append(((w * cols + t) * 2 + s, target))
        return lax.ppermute(value, axes, pairs)

    order = list(range(wide - 1, 0, -1))
    packed = call(
        functools.partial(pack_kernel, wide, cols),
        (core_lists, labels, head_embed, tail_embed),
        [(block, half + depth)] * (wide - 1) + [(depth + rows + 8, half), (block, dim), (block, depth)],
        scalars=1,
    )
    z_out, x_out, head_own, label_own = packed[: wide - 1], packed[-3], packed[-2], packed[-1]
    z_in, z_swap = {}, {}
    for k in order:
        got = []
        for j in range(max(1, cols // 2)):
            sent = z_out[k - 1] if j == 0 else z_out[k - 1][:, half:]
            got.append(move(sent, k, (2 * j, (2 * j + 1) % cols)))
        z_in[k] = got
    x_in = [move(x_out, 0, (o, o)) for o in range(1, cols)]
    (query,) = call(
        query_kernel, (core_mats, tail_embed, *x_in), [(dim, cols * depth)], flops=6 * dim * half * cols * depth
    )
    query_other = move(query, 0, flip=1)
    for k in order:
        z_swap[k] = [move(value, 0, flip=1) for value in z_in[k]]

    per = len(z_in[1])
    flat_in = [value for k in range(1, wide) for value in z_in[k]]
    flat_swap = [value for k in range(1, wide) for value in z_swap[k]]
    core_rows, tail_rows = dim // wide, depth // wide
    chunks = cols * depth // half
    small = dim // half * chunk + -(-tail_rows // 8) * 8
    send_shape = (chunks * core_rows // 2 + small, half)
    own_shape = (chunks * core_rows + small, half)

    def grads(list_ref, core_ref, query_ref, other_ref, head_ref, label_ref, *rest):
        x_refs, rest = rest[: cols - 1], rest[cols - 1 :]
        count = len(flat_in)
        group = lambda refs: [refs[i : i + per] for i in range(0, count, per)]
        z_refs, swap_refs, rest = group(rest[:count]), group(rest[count : 2 * count]), rest[2 * count :]
        outs, own_ref, scratch = rest[: wide - 1], rest[wide - 1], rest[wide:]
        grad_kernel(
            wide, cols,
            (list_ref, core_ref, query_ref, other_ref, head_ref, label_ref, x_refs, z_refs, swap_refs, outs, own_ref)
            + tuple(scratch),
        )

    made = call(
        grads,
        (core_lists, core_mats, query, query_other, head_own, label_own, *x_in, *flat_in, *flat_swap),
        [send_shape] * (wide - 1) + [own_shape],
        scratch=[(wide * block, dim), (wide * block, cols * depth), (dim, cols * depth), (depth, half)],
        scalars=1,
        flops=6 * wide * block * dim * cols * depth * 2,
    )
    own = made[-1]
    back = {k: move(made[k - 1], k) for k in order}
    back_swap = {k: move(back[k], 0, flip=1) for k in order}
    heads_total, tails_total = block * wide, depth * cols
    scales = (
        1.0 / math.sqrt(slots * tails_total),
        1.0 / math.sqrt(slots * heads_total),
        1.0 / math.sqrt(heads_total * depth),
    )
    each = wide // cols

    def finish(tail_ref, *rest):
        x_refs, rest = rest[: cols - 1], rest[cols - 1 :]
        finish_kernel(
            wide, cols, scales, tail_ref, x_refs, rest[0], rest[1:wide], rest[wide : 2 * wide - 1], *rest[2 * wide - 1 :]
        )

    return call(
        finish,
        (tail_embed, *x_in, own, *[back[k] for k in range(1, wide)], *[back_swap[k] for k in range(1, wide)]),
        [(chunk, dim), (1, tail_rows, half), (each, core_rows, half)],
        scratch=[(each, core_rows, cols * depth)],
        flops=6 * each * core_rows * cols * depth * half,
    )


def solution(mesh):
    in_specs = (
        P(("groups", "wide"), None),
        P(("groups", "tail"), "sub"),
        P(("groups", "wide"), None, "sub"),
        P(("groups", "wide"), None, "tail"),
        P(("groups", "tail"), None),
    )
    out_specs = (
        P(("groups", "wide", "tail", "sub"), None),
        P(("groups", "tail"), "wide", "sub"),
        P(("groups", "tail"), "wide", "sub"),
    )
    return jax.shard_map(body, mesh=mesh, in_specs=in_specs, out_specs=out_specs, check_vma=False)
```

```python
import functools
import math

import jax
import jax.numpy as jnp
from jax import lax
from jax.experimental import pallas as pl
from jax.experimental.pallas import tpu as pltpu
from jax.sharding import PartitionSpec as P


F32 = jnp.float32
VMEM_LIMIT = 48 * 1024 * 1024
QUERY_PARTS = 4
FULL_LIMIT = 62 * 1024 * 1024
NN = (((1,), (0,)), ((), ()))
NT = (((1,), (1,)), ((), ()))
TN = (((0,), (0,)), ((), ()))


def split(value):
    high = value.astype(jnp.bfloat16)
    low = (value - high.astype(F32)).astype(jnp.bfloat16)
    return high, low


def dot3(left, right, dims):
    lh, ll = left
    rh, rl = right
    mul = functools.partial(lax.dot_general, dimension_numbers=dims, preferred_element_type=F32)
    return mul(lh, rh) + (mul(lh, rl) + mul(ll, rh))


def rows_at(ref, index, count):
    if count % 8 == 0:
        return ref[pl.ds(pl.multiple_of(index * count, count), count), :]
    per = 8 // count
    window = ref[pl.ds(pl.multiple_of(index // per * 8, 8), 8), :]
    found = window[0:count]
    for i in range(1, per):
        found = jnp.where(index % per == i, window[i * count : (i + 1) * count], found)
    return found


def place():
    return lax.axis_index("wide"), lax.axis_index("tail"), lax.axis_index("sub")


def pack_kernel(wide, cols, list_hbm, label_hbm, head_hbm, tail_hbm, *refs):
    z_refs, (x_ref, head_own, label_own, listed, label_ref, head_ref, sems) = refs[: wide - 1], refs[wide - 1 :]
    w, t, s = place()
    block, slots, width = label_ref.shape
    chunk = block // (2 * cols)
    rows = block // 2
    depth, half = tail_hbm.shape
    copies = [
        pltpu.make_async_copy(source, target, sems.at[i])
        for i, (source, target) in enumerate(
            ((list_hbm, listed), (label_hbm, label_ref), (head_hbm, head_ref), (tail_hbm, x_ref.at[0:depth]))
        )
    ]
    for copy in copies:
        copy.start()
    copies[0].wait()
    count = jnp.int32(0)
    for j in range(slots):
        count = count + (listed[0, j] == w).astype(jnp.int32)
    x_ref[depth + rows :, :] = jnp.full((8, half), count.astype(F32), F32)
    label_own[block:, :] = jnp.full((8, width), count.astype(F32), F32)
    copies[1].wait()
    copies[2].wait()
    for part in range(2):
        for col in range(cols):
            start = pl.multiple_of((col * 2 + (s ^ part)) * chunk, chunk)
            at = part * rows + col * chunk
            embed = head_ref[pl.ds(start, chunk), :]
            head_own[at : at + chunk, :] = embed
            slot_labels = [label_ref[pl.ds(start, chunk), j, :] for j in range(slots)]
            for k in range(wide):
                total = jnp.zeros((chunk, width), jnp.int32)
                for j in range(slots):
                    total = total + jnp.where(listed[0, j] == (w ^ k), slot_labels[j], 0)
                total = total.astype(F32)
                if k == 0:
                    label_own[at : at + chunk, :] = total
                    lane = (at // rows) * width
                    row = depth + at % rows
                    x_ref[row : row + chunk, lane : lane + width] = total
                else:
                    z_refs[k - 1][at : at + chunk, half : half + width] = total
                    if part == 0:
                        z_refs[k - 1][at : at + chunk, 0:half] = embed[:, 0:half]
                        z_refs[k - 1][rows + at : rows + at + chunk, 0:half] = embed[:, half:]
    copies[3].wait()


def query_kernel(core_ref, tail_ref, *refs):
    x_refs, outs = refs[: -1 - QUERY_PARTS], refs[-QUERY_PARTS:]
    depth = tail_ref.shape[0]
    tails = [tail_ref[...]] + [x[0:depth, :] for x in x_refs]
    value = dot3(split(core_ref[0]), split(jnp.concatenate(tails, axis=0)), NT)
    size = outs[0].shape[0]
    for i, ref in enumerate(outs):
        ref[...] = value[i * size : (i + 1) * size]


def grad_kernel(wide, cols, refs):
    (core_ref, query_refs, query_others, head_own, label_own, x_refs, z_refs, swap_refs, outs, own_ref,
     heads, resid, outer, tails) = refs
    w, t, s = place()
    block, dim = head_own.shape
    width = label_own.shape[1]
    rows = block // 2
    chunk = rows // cols
    half = core_ref.shape[2]
    heads[0:block, :] = head_own[...]
    for k in range(1, wide):
        at = k * block
        for part, ref in enumerate((z_refs[k - 1][0], swap_refs[k - 1][0])):
            heads[at + part * rows : at + part * rows + rows, 0:half] = ref[0:rows, 0:half]
            heads[at + part * rows : at + part * rows + rows, half:] = ref[rows:, 0:half]
    query = split(jnp.concatenate([a[...] + b[...] for a, b in zip(query_refs, query_others)], axis=0))
    head_parts = split(heads[...])
    score = dot3(head_parts, query, NN)
    prob = jax.nn.sigmoid(score)
    depth = x_refs[0].shape[0] - 8 - rows if x_refs else 0
    for o in range(cols):
        lanes = slice(o * width, (o + 1) * width)
        times = label_own[block : block + 1, :] if o == 0 else x_refs[o - 1][depth + rows : depth + rows + 1, 0:width]
        if o == 0:
            resid[0:block, lanes] = times * prob[0:block, lanes] - label_own[0:block, :]
        else:
            ref = x_refs[o - 1]
            for part in range(2):
                resid[part * rows : part * rows + rows, lanes] = (
                    times * prob[part * rows : part * rows + rows, lanes]
                    - ref[depth : depth + rows, part * width : (part + 1) * width]
                )
        for k in range(1, wide):
            first, last = (half, half + width) if o < 2 else (0, width)
            mine = z_refs[k - 1][o // 2][:, first:last]
            other = swap_refs[k - 1][o // 2]
            other = jnp.concatenate([other[rows:, first:last], other[0:rows, first:last]], axis=0)
            label = jnp.where(s == o % 2, mine, other)
            resid[k * block : (k + 1) * block, lanes] = times * prob[k * block : (k + 1) * block, lanes] - label
    resid_parts = split(resid[...])
    outer[...] = dot3(head_parts, resid_parts, TN)
    tails[...] = dot3(split(outer[:, 0:width]), split(core_ref[0]), TN)
    picked = [resid[pl.ds(pl.multiple_of(k * block + t * chunk, chunk), chunk), :] for k in range(wide)]
    head_sum = dot3(split(jnp.concatenate(picked, axis=0)), query, NT)
    core_rows = dim // wide
    tail_rows = width // wide
    span = core_rows // 2
    chunks = cols * width // half
    for k in range(wide):
        ref = own_ref if k == 0 else outs[k - 1]
        take = core_rows if k == 0 else span
        start = (w ^ k) * core_rows if k == 0 else (w ^ k) * core_rows + s * span
        piece = outer[pl.ds(pl.multiple_of(start, take), take), :]
        at = 0
        for i in range(chunks):
            ref[at : at + take, :] = piece[:, i * half : (i + 1) * half]
            at += take
        for i in range(dim // half):
            ref[at : at + chunk, :] = head_sum[k * chunk : (k + 1) * chunk, i * half : (i + 1) * half]
            at += chunk
        ref[at : at + tail_rows, :] = rows_at(tails, w ^ k, tail_rows)


def finish_kernel(wide, cols, scales, tail_ref, x_refs, own_ref, z_refs, swap_refs, head_out, tail_out, core_out, pieces):
    w, t, s = place()
    depth, half = tail_ref.shape
    core_rows = core_out.shape[1]
    span = core_rows // 2
    chunk, dim = head_out.shape
    tail_rows = tail_out.shape[1]
    chunks = cols * depth // half
    each = wide // cols
    for k in range(wide):
        relation = w ^ k

        @pl.when(relation // each == t)
        def _(k=k, at=relation % each):
            for i in range(chunks):
                lanes = slice(i * half, (i + 1) * half)
                if k == 0:
                    pieces[at, :, lanes] = own_ref[i * core_rows : (i + 1) * core_rows, :]
                else:
                    pieces[at, pl.ds(pl.multiple_of(s * span, span), span), lanes] = (
                        z_refs[k - 1][i * span : (i + 1) * span, :]
                    )
                    pieces[at, pl.ds(pl.multiple_of((1 - s) * span, span), span), lanes] = (
                        swap_refs[k - 1][i * span : (i + 1) * span, :]
                    )

    tails = split(jnp.concatenate([tail_ref[...]] + [x[0:depth, :] for x in x_refs], axis=0))
    for i in range(each):
        core_out[i] = dot3(split(pieces[i]), tails, NN) * scales[2]
    for i in range(dim // half):
        at = chunks * core_rows + i * chunk
        total = own_ref[at : at + chunk, :]
        for ref in z_refs:
            at = chunks * span + i * chunk
            total = total + ref[at : at + chunk, :]
        head_out[:, i * half : (i + 1) * half] = total * scales[0]
    at = chunks * core_rows + dim // half * chunk
    total = own_ref[at : at + tail_rows, :]
    for ref in z_refs:
        at = chunks * span + dim // half * chunk
        total = total + ref[at : at + tail_rows, :]
    tail_out[0] = total * scales[1]


def call(kernel, inputs, outputs, scratch=(), hbm=(), flops=0, limit=VMEM_LIMIT):
    vmem, far = pl.BlockSpec(memory_space=pltpu.VMEM), pl.BlockSpec(memory_space=pltpu.HBM)
    return pl.pallas_call(
        kernel,
        out_shape=tuple(jax.ShapeDtypeStruct(shape, F32) for shape in outputs),
        in_specs=[far if i in hbm else vmem for i in range(len(inputs))],
        out_specs=tuple(vmem for _ in outputs),
        scratch_shapes=[pltpu.VMEM(item, F32) if isinstance(item, tuple) else item for item in scratch],
        compiler_params=pltpu.CompilerParams(vmem_limit_bytes=limit),
        cost_estimate=pl.CostEstimate(flops=flops, bytes_accessed=4 * sum(x.size for x in inputs), transcendentals=0),
    )(*inputs)


def body(head_embed, tail_embed, core_mats, labels, core_lists):
    wide, cols = lax.axis_size("wide"), lax.axis_size("tail")
    block, dim = head_embed.shape
    depth, half = tail_embed.shape
    slots = core_lists.shape[1]
    rows = block // 2
    chunk = rows // cols
    axes = ("wide", "tail", "sub")

    def move(value, k, offsets=(0, 0), flip=0):
        pairs = []
        for w in range(wide):
            for t in range(cols):
                for s in range(2):
                    target = ((w ^ k) * cols + (t ^ offsets[s])) * 2 + (s ^ flip)
                    pairs.append(((w * cols + t) * 2 + s, target))
        return lax.ppermute(value, axes, pairs)

    order = list(range(wide - 1, 0, -1))
    packed = call(
        functools.partial(pack_kernel, wide, cols),
        (core_lists, labels, head_embed, tail_embed),
        [(block, half + depth)] * (wide - 1) + [(depth + rows + 8, half), (block, dim), (block + 8, depth)],
        scratch=[
            pltpu.SMEM(core_lists.shape, jnp.int32),
            pltpu.VMEM(labels.shape, jnp.int32),
            head_embed.shape,
            pltpu.SemaphoreType.DMA((4,)),
        ],
        hbm=range(4),
        limit=FULL_LIMIT,
    )
    z_out, x_out, head_own, label_own = packed[: wide - 1], packed[-3], packed[-2], packed[-1]
    z_in, z_swap = {}, {}
    for k in order:
        got = []
        for j in range(max(1, cols // 2)):
            sent = z_out[k - 1] if j == 0 else z_out[k - 1][:, half:]
            got.append(move(sent, k, (2 * j, (2 * j + 1) % cols)))
        z_in[k] = got
    x_in = [move(x_out, 0, (o, o)) for o in range(1, cols)]
    query = call(
        query_kernel,
        (core_mats, tail_embed, *x_in, z_in[order[0]][0]),
        [(dim // QUERY_PARTS, cols * depth)] * QUERY_PARTS,
        hbm=(cols + 1,),
        flops=6 * dim * half * cols * depth,
    )
    query_other = [move(value, 0, flip=1) for value in query]
    for k in order:
        z_swap[k] = [move(value, 0, flip=1) for value in z_in[k]]

    per = len(z_in[1])
    flat_in = [value for k in range(1, wide) for value in z_in[k]]
    flat_swap = [value for k in range(1, wide) for value in z_swap[k]]
    core_rows, tail_rows = dim // wide, depth // wide
    chunks = cols * depth // half
    small = dim // half * chunk + -(-tail_rows // 8) * 8
    send_shape = (chunks * core_rows // 2 + small, half)
    own_shape = (chunks * core_rows + small, half)

    def grads(core_ref, *rest):
        query_refs, other_refs, rest = rest[:QUERY_PARTS], rest[QUERY_PARTS : 2 * QUERY_PARTS], rest[2 * QUERY_PARTS :]
        head_ref, label_ref, *rest = rest
        x_refs, rest = rest[: cols - 1], rest[cols - 1 :]
        count = len(flat_in)
        group = lambda refs: [refs[i : i + per] for i in range(0, count, per)]
        z_refs, swap_refs, rest = group(rest[:count]), group(rest[count : 2 * count]), rest[2 * count :]
        outs, own_ref, scratch = rest[: wide - 1], rest[wide - 1], rest[wide:]
        grad_kernel(
            wide, cols,
            (core_ref, query_refs, other_refs, head_ref, label_ref, x_refs, z_refs, swap_refs, outs, own_ref)
            + tuple(scratch),
        )

    made = call(
        grads,
        (core_mats, *query, *query_other, head_own, label_own, *x_in, *flat_in, *flat_swap),
        [send_shape] * (wide - 1) + [own_shape],
        scratch=[(wide * block, dim), (wide * block, cols * depth), (dim, cols * depth), (depth, half)],
        flops=6 * wide * block * dim * cols * depth * 2,
    )
    own = made[-1]
    back = {k: move(made[k - 1], k) for k in order}
    back_swap = {k: move(back[k], 0, flip=1) for k in order}
    heads_total, tails_total = block * wide, depth * cols
    scales = (
        1.0 / math.sqrt(slots * tails_total),
        1.0 / math.sqrt(slots * heads_total),
        1.0 / math.sqrt(heads_total * depth),
    )
    each = wide // cols

    def finish(tail_ref, *rest):
        x_refs, rest = rest[: cols - 1], rest[cols - 1 :]
        finish_kernel(
            wide, cols, scales, tail_ref, x_refs, rest[0], rest[1:wide], rest[wide : 2 * wide - 1], *rest[2 * wide - 1 :]
        )

    return call(
        finish,
        (tail_embed, *x_in, own, *[back[k] for k in range(1, wide)], *[back_swap[k] for k in range(1, wide)]),
        [(chunk, dim), (1, tail_rows, half), (each, core_rows, half)],
        scratch=[(each, core_rows, cols * depth)],
        flops=6 * each * core_rows * cols * depth * half,
    )


def solution(mesh):
    in_specs = (
        P(("groups", "wide"), None),
        P(("groups", "tail"), "sub"),
        P(("groups", "wide"), None, "sub"),
        P(("groups", "wide"), None, "tail"),
        P(("groups", "tail"), None),
    )
    out_specs = (
        P(("groups", "wide", "tail", "sub"), None),
        P(("groups", "tail"), "wide", "sub"),
        P(("groups", "tail"), "wide", "sub"),
    )
    return jax.shard_map(body, mesh=mesh, in_specs=in_specs, out_specs=out_specs, check_vma=False)
```

```python
import functools
import math

import jax
import jax.numpy as jnp
from jax import lax
from jax.experimental import pallas as pl
from jax.experimental.pallas import tpu as pltpu
from jax.sharding import PartitionSpec as P


F32 = jnp.float32
VMEM_LIMIT = 48 * 1024 * 1024
QUERY_PARTS = 4
FULL_LIMIT = 62 * 1024 * 1024
NN = (((1,), (0,)), ((), ()))
NT = (((1,), (1,)), ((), ()))
TN = (((0,), (0,)), ((), ()))


def split(value):
    high = value.astype(jnp.bfloat16)
    low = (value - high.astype(F32)).astype(jnp.bfloat16)
    return high, low


def dot3(left, right, dims):
    lh, ll = left
    rh, rl = right
    mul = functools.partial(lax.dot_general, dimension_numbers=dims, preferred_element_type=F32)
    return mul(lh, rh) + (mul(lh, rl) + mul(ll, rh))


def rows_at(ref, index, count):
    if count % 8 == 0:
        return ref[pl.ds(pl.multiple_of(index * count, count), count), :]
    per = 8 // count
    window = ref[pl.ds(pl.multiple_of(index // per * 8, 8), 8), :]
    found = window[0:count]
    for i in range(1, per):
        found = jnp.where(index % per == i, window[i * count : (i + 1) * count], found)
    return found


def place():
    return lax.axis_index("wide"), lax.axis_index("tail"), lax.axis_index("sub")


def pack_kernel(wide, cols, list_hbm, label_hbm, head_hbm, tail_hbm, *refs):
    z_refs, (x_ref, head_own, label_own, listed, label_ref, head_ref, sems) = refs[: wide - 1], refs[wide - 1 :]
    w, t, s = place()
    block, slots, width = label_ref.shape
    chunk = block // (2 * cols)
    rows = block // 2
    depth, half = tail_hbm.shape
    copies = [
        pltpu.make_async_copy(source, target, sems.at[i])
        for i, (source, target) in enumerate(
            ((list_hbm, listed), (label_hbm, label_ref), (head_hbm, head_ref), (tail_hbm, x_ref.at[0:depth]))
        )
    ]
    for copy in copies:
        copy.start()
    copies[0].wait()
    count = jnp.int32(0)
    for j in range(slots):
        count = count + (listed[0, j] == w).astype(jnp.int32)
    x_ref[depth + rows :, :] = jnp.full((8, half), count.astype(F32), F32)
    label_own[block:, :] = jnp.full((8, width), count.astype(F32), F32)
    copies[1].wait()
    copies[2].wait()
    for part in range(2):
        for col in range(cols):
            start = pl.multiple_of((col * 2 + (s ^ part)) * chunk, chunk)
            at = part * rows + col * chunk
            embed = head_ref[pl.ds(start, chunk), :]
            head_own[at : at + chunk, :] = embed
            slot_labels = [label_ref[pl.ds(start, chunk), j, :] for j in range(slots)]
            for k in range(wide):
                total = jnp.zeros((chunk, width), jnp.int32)
                for j in range(slots):
                    total = total + jnp.where(listed[0, j] == (w ^ k), slot_labels[j], 0)
                total = total.astype(F32)
                if k == 0:
                    label_own[at : at + chunk, :] = total
                    lane = (at // rows) * width
                    row = depth + at % rows
                    x_ref[row : row + chunk, lane : lane + width] = total
                else:
                    z_refs[k - 1][at : at + chunk, half : half + width] = total
                    if part == 0:
                        z_refs[k - 1][at : at + chunk, 0:half] = embed[:, 0:half]
                        z_refs[k - 1][rows + at : rows + at + chunk, 0:half] = embed[:, half:]
    copies[3].wait()


def query_kernel(core_ref, tail_ref, *refs):
    x_refs, outs = refs[: -2 - QUERY_PARTS], refs[-QUERY_PARTS:]
    depth = tail_ref.shape[0]
    tails = [tail_ref[...]] + [x[0:depth, :] for x in x_refs]
    value = dot3(split(core_ref[0]), split(jnp.concatenate(tails, axis=0)), NT)
    size = outs[0].shape[0]
    for i, ref in enumerate(outs):
        ref[...] = value[i * size : (i + 1) * size]


def grad_kernel(wide, cols, refs):
    (core_ref, core_other, query_refs, query_others, head_own, label_own, x_refs, z_refs, swap_refs, own_ref, joint_ref, fars,
     heads, resid, outer, tails, tails_other) = refs
    w, t, s = place()
    block, dim = head_own.shape
    width = label_own.shape[1]
    rows = block // 2
    chunk = rows // cols
    half = core_ref.shape[2]
    heads[0:block, :] = head_own[...]
    for k in range(1, wide):
        at = k * block
        for part, ref in enumerate((z_refs[k - 1][0], swap_refs[k - 1][0])):
            heads[at + part * rows : at + part * rows + rows, 0:half] = ref[0:rows, 0:half]
            heads[at + part * rows : at + part * rows + rows, half:] = ref[rows:, 0:half]
    query = split(jnp.concatenate([a[...] + b[...] for a, b in zip(query_refs, query_others)], axis=0))
    head_parts = split(heads[...])
    score = dot3(head_parts, query, NN)
    prob = jax.nn.sigmoid(score)
    depth = x_refs[0].shape[0] - 8 - rows if x_refs else 0
    for o in range(cols):
        lanes = slice(o * width, (o + 1) * width)
        times = label_own[block : block + 1, :] if o == 0 else x_refs[o - 1][depth + rows : depth + rows + 1, 0:width]
        if o == 0:
            resid[0:block, lanes] = times * prob[0:block, lanes] - label_own[0:block, :]
        else:
            ref = x_refs[o - 1]
            for part in range(2):
                resid[part * rows : part * rows + rows, lanes] = (
                    times * prob[part * rows : part * rows + rows, lanes]
                    - ref[depth : depth + rows, part * width : (part + 1) * width]
                )
        for k in range(1, wide):
            first, last = (half, half + width) if o < 2 else (0, width)
            mine = z_refs[k - 1][o // 2][:, first:last]
            other = swap_refs[k - 1][o // 2]
            other = jnp.concatenate([other[rows:, first:last], other[0:rows, first:last]], axis=0)
            label = jnp.where(s == o % 2, mine, other)
            resid[k * block : (k + 1) * block, lanes] = times * prob[k * block : (k + 1) * block, lanes] - label
    resid_parts = split(resid[...])
    outer[...] = dot3(head_parts, resid_parts, TN)
    tails[...] = dot3(split(outer[...]), split(core_ref[0]), TN)
    across = jnp.where(s == 0, outer[:, 0:width], outer[:, width : 2 * width])
    tails_other[...] = dot3(split(across), split(core_other[0]), TN)
    starts = [k * block + t * chunk for k in range(2)]
    for j in range(1, wide // 2):
        starts += [(2 * j + 1 - s) * block + part * rows + (t ^ s) * chunk for part in range(2)]
    picked = [resid[pl.ds(pl.multiple_of(start, chunk), chunk), :] for start in starts]
    head_sum = dot3(split(jnp.concatenate(picked, axis=0)), query, NT)
    core_rows = dim // wide
    tail_rows = width // wide
    span = core_rows // 2

    def put_outer(ref, start, take, flip):
        piece = outer[pl.ds(pl.multiple_of(start, take), take), :]
        for i in range(cols // 2):
            first, last = piece[:, 2 * i * width : (2 * i + 1) * width], piece[:, (2 * i + 1) * width : 2 * (i + 1) * width]
            if flip:
                first, last = jnp.where(s == 0, first, last), jnp.where(s == 0, last, first)
            ref[i * take : (i + 1) * take, 0:width] = first
            ref[i * take : (i + 1) * take, width:] = last
        return cols // 2 * take

    def put_head(ref, at, item):
        for i in range(dim // half):
            ref[at : at + chunk, :] = head_sum[item * chunk : (item + 1) * chunk, i * half : (i + 1) * half]
            at += chunk
        return at

    for k, ref in enumerate((own_ref, joint_ref)):
        take = core_rows if k == 0 else span
        at = put_outer(ref, (w ^ k) * core_rows + (0 if k == 0 else s * span), take, False)
        at = put_head(ref, at, k)
        ref[at : at + tail_rows, :] = rows_at(tails, w ^ k, tail_rows)
    for j, (outer_ref, sum_ref) in enumerate(fars, 1):
        target = w ^ (2 * j + 1 - s)
        put_outer(outer_ref, target * core_rows, core_rows, True)
        at = put_head(sum_ref, put_head(sum_ref, 0, 2 * j), 2 * j + 1)
        pitch = -(-tail_rows // 8) * 8
        sum_ref[at : at + tail_rows, :] = rows_at(tails, s * wide + target, tail_rows)
        sum_ref[at + pitch : at + pitch + tail_rows, :] = rows_at(tails_other, target, tail_rows)


def finish_kernel(wide, cols, scales, tail_ref, x_refs, own_ref, joint, fars, head_out, tail_out, core_out, pieces):
    w, t, s = place()
    depth, half = tail_ref.shape
    core_rows = core_out.shape[1]
    span = core_rows // 2
    chunk, dim = head_out.shape
    tail_rows = tail_out.shape[1]
    chunks = cols * depth // half
    each = wide // cols

    def keep(relation, parts):
        @pl.when(relation // each == t)
        def _():
            at = relation % each
            for ref, start, take in parts:
                for i in range(chunks):
                    pieces[at, pl.ds(pl.multiple_of(start, take), take), i * half : (i + 1) * half] = (
                        ref[i * take : (i + 1) * take, :]
                    )

    keep(w, [(own_ref, 0, core_rows)])
    keep(w ^ 1, [(joint[0], s * span, span), (joint[1], (1 - s) * span, span)])
    lead = [(own_ref, chunks * core_rows, 0), (joint[0], chunks * span, 0)]
    for j, (outer_in, outer_swap, sum_in, sum_swap) in enumerate(fars, 1):
        keep(w ^ (2 * j + 1 - s), [(outer_in, 0, core_rows)])
        keep(w ^ (2 * j + s), [(outer_swap, 0, core_rows)])
        lead += [(sum_in, 0, 0), (sum_swap, 0, 1)]
    heads = dim // half * chunk
    pitch = -(-tail_rows // 8) * 8
    for i in range(dim // half):
        total = sum(ref[at + part * heads + i * chunk : at + part * heads + (i + 1) * chunk, :] for ref, at, part in lead)
        head_out[:, i * half : (i + 1) * half] = total * scales[0]
    total = 0.0
    for n, (ref, at, part) in enumerate(lead):
        at += heads if n < 2 else 2 * heads + part * pitch
        total = total + ref[at : at + tail_rows, :]
    tail_out[0] = total * scales[1]
    tails = split(jnp.concatenate([tail_ref[...]] + [x[0:depth, :] for x in x_refs], axis=0))
    for i in range(each):
        core_out[i] = dot3(split(pieces[i]), tails, NN) * scales[2]


def call(kernel, inputs, outputs, scratch=(), hbm=(), flops=0, limit=VMEM_LIMIT):
    vmem, far = pl.BlockSpec(memory_space=pltpu.VMEM), pl.BlockSpec(memory_space=pltpu.HBM)
    return pl.pallas_call(
        kernel,
        out_shape=tuple(jax.ShapeDtypeStruct(shape, F32) for shape in outputs),
        in_specs=[far if i in hbm else vmem for i in range(len(inputs))],
        out_specs=tuple(vmem for _ in outputs),
        scratch_shapes=[pltpu.VMEM(item, F32) if isinstance(item, tuple) else item for item in scratch],
        compiler_params=pltpu.CompilerParams(vmem_limit_bytes=limit),
        cost_estimate=pl.CostEstimate(flops=flops, bytes_accessed=4 * sum(x.size for x in inputs), transcendentals=0),
    )(*inputs)


def body(head_embed, tail_embed, core_mats, labels, core_lists):
    wide, cols = lax.axis_size("wide"), lax.axis_size("tail")
    block, dim = head_embed.shape
    depth, half = tail_embed.shape
    slots = core_lists.shape[1]
    rows = block // 2
    chunk = rows // cols
    axes = ("wide", "tail", "sub")

    def move(value, k, offsets=(0, 0), flip=0, owners=False):
        steps = k if isinstance(k, tuple) else (k, k)
        pairs = []
        for w in range(wide):
            for t in range(cols):
                for s in range(2):
                    line = t ^ offsets[s]
                    if not owners or line == w // (wide // cols):
                        target = ((w ^ steps[s]) * cols + line) * 2 + (s ^ flip)
                        pairs.append(((w * cols + t) * 2 + s, target))
        return lax.ppermute(value, axes, pairs)

    order = list(range(wide - 1, 0, -1))
    core_other = move(core_mats, 0, flip=1)
    packed = call(
        functools.partial(pack_kernel, wide, cols),
        (core_lists, labels, head_embed, tail_embed),
        [(block, half + depth)] * (wide - 1) + [(depth + rows + 8, half), (block, dim), (block + 8, depth)],
        scratch=[
            pltpu.SMEM(core_lists.shape, jnp.int32),
            pltpu.VMEM(labels.shape, jnp.int32),
            head_embed.shape,
            pltpu.SemaphoreType.DMA((4,)),
        ],
        hbm=range(4),
        limit=FULL_LIMIT,
    )
    z_out, x_out, head_own, label_own = packed[: wide - 1], packed[-3], packed[-2], packed[-1]
    z_in, z_swap = {}, {}
    for k in order:
        got = []
        for j in range(max(1, cols // 2)):
            sent = z_out[k - 1] if j == 0 else z_out[k - 1][:, half:]
            got.append(move(sent, k, (2 * j, (2 * j + 1) % cols)))
        z_in[k] = got
    x_in = [move(x_out, 0, (o, o)) for o in range(1, cols)]
    query = call(
        query_kernel,
        (core_mats, tail_embed, *x_in, z_in[order[0]][0], core_other),
        [(dim // QUERY_PARTS, cols * depth)] * QUERY_PARTS,
        hbm=(cols + 1, cols + 2),
        flops=6 * dim * half * cols * depth,
    )
    query_other = [move(value, 0, flip=1) for value in query]
    for k in order:
        ready = z_in[k] if k == order[0] else lax.optimization_barrier((z_in[k], query[0]))[0]
        z_swap[k] = [move(value, 0, flip=1) for value in ready]

    per = len(z_in[1])
    flat_in = [value for k in range(1, wide) for value in z_in[k]]
    flat_swap = [value for k in range(1, wide) for value in z_swap[k]]
    core_rows, tail_rows = dim // wide, depth // wide
    chunks = cols * depth // half
    small = dim // half * chunk + -(-tail_rows // 8) * 8
    own_shape = (chunks * core_rows + small, half)
    joint_shape = (chunks * core_rows // 2 + small, half)
    pairs = range(1, wide // 2)

    def grads(core_ref, other_ref, *rest):
        query_refs, query_others, rest = rest[:QUERY_PARTS], rest[QUERY_PARTS : 2 * QUERY_PARTS], rest[2 * QUERY_PARTS :]
        head_ref, label_ref, *rest = rest
        x_refs, rest = rest[: cols - 1], rest[cols - 1 :]
        count = len(flat_in)
        group = lambda refs: [refs[i : i + per] for i in range(0, count, per)]
        z_refs, swap_refs, rest = group(rest[:count]), group(rest[count : 2 * count]), rest[2 * count :]
        own_ref, joint_ref, rest = rest[0], rest[1], rest[2:]
        fars, scratch = list(zip(rest[0 : 2 * len(pairs) : 2], rest[1 : 2 * len(pairs) : 2])), rest[2 * len(pairs) :]
        grad_kernel(
            wide, cols,
            (core_ref, other_ref, query_refs, query_others, head_ref, label_ref, x_refs, z_refs, swap_refs, own_ref, joint_ref, fars)
            + tuple(scratch),
        )

    made = call(
        grads,
        (core_mats, core_other, *query, *query_other, head_own, label_own, *x_in, *flat_in, *flat_swap),
        [own_shape, joint_shape] + [(chunks * core_rows, half), (2 * small, half)] * len(pairs),
        scratch=[
            (wide * block, dim), (wide * block, cols * depth), (dim, cols * depth), (cols * depth, half), (depth, half),
        ],
        flops=6 * wide * block * dim * cols * depth * 2,
    )
    own, far = made[0], []
    for j in pairs:
        steps = (2 * j + 1, 2 * j)
        far.append([move(made[2 * j], steps, (0, 1), owners=True), move(made[2 * j + 1], steps, (0, 1))])
    joint = move(made[1], 1)
    far = [(a, move(a, 0, flip=1), b, move(b, 0, flip=1)) for a, b in far]
    joint_swap = move(joint, 0, flip=1)
    heads_total, tails_total = block * wide, depth * cols
    scales = (
        1.0 / math.sqrt(slots * tails_total),
        1.0 / math.sqrt(slots * heads_total),
        1.0 / math.sqrt(heads_total * depth),
    )
    each = wide // cols

    def finish(tail_ref, *rest):
        x_refs, rest = rest[: cols - 1], rest[cols - 1 :]
        own_ref, rest = rest[0], rest[1:]
        far_s, rest = rest[: 2 * len(pairs)], rest[2 * len(pairs) :]
        joint_refs, rest = rest[:2], rest[2:]
        far_u, rest = rest[: 2 * len(pairs)], rest[2 * len(pairs) :]
        fars = [far_u[2 * i : 2 * i + 2] + far_s[2 * i : 2 * i + 2] for i in range(len(pairs))]
        finish_kernel(wide, cols, scales, tail_ref, x_refs, own_ref, joint_refs, fars, *rest)

    return call(
        finish,
        (tail_embed, *x_in, own, *[v for g in far for v in g[2:]], joint, joint_swap, *[v for g in far for v in g[:2]]),
        [(chunk, dim), (1, tail_rows, half), (each, core_rows, half)],
        scratch=[(each, core_rows, cols * depth)],
        flops=6 * each * core_rows * cols * depth * half,
    )


def solution(mesh):
    in_specs = (
        P(("groups", "wide"), None),
        P(("groups", "tail"), "sub"),
        P(("groups", "wide"), None, "sub"),
        P(("groups", "wide"), None, "tail"),
        P(("groups", "tail"), None),
    )
    out_specs = (
        P(("groups", "wide", "tail", "sub"), None),
        P(("groups", "tail"), "wide", "sub"),
        P(("groups", "tail"), "wide", "sub"),
    )
    return jax.shard_map(body, mesh=mesh, in_specs=in_specs, out_specs=out_specs, check_vma=False)
```

```python
import functools
import math

import jax
import jax.numpy as jnp
from jax import lax
from jax.experimental import pallas as pl
from jax.experimental.pallas import tpu as pltpu
from jax.sharding import PartitionSpec as P


F32 = jnp.float32
VMEM_LIMIT = 48 * 1024 * 1024
FULL_LIMIT = 62 * 1024 * 1024
NN = (((1,), (0,)), ((), ()))
NT = (((1,), (1,)), ((), ()))
TN = (((0,), (0,)), ((), ()))


def split(value):
    high = value.astype(jnp.bfloat16)
    low = (value - high.astype(F32)).astype(jnp.bfloat16)
    return high, low


def dot3(left, right, dims):
    lh, ll = left
    rh, rl = right
    mul = functools.partial(lax.dot_general, dimension_numbers=dims, preferred_element_type=F32)
    free = 1 - dims[0][0][0]
    size = lh.shape[free]
    both = mul(jnp.concatenate([lh, ll], axis=free), rh)
    return both[:size] + (mul(lh, rl) + both[size:])


def window(ref, index, count):
    size = max(count, 8)
    return ref[pl.ds(pl.multiple_of(index * count // size * size, size), size), :]


def pick(value, index, count):
    if count % 8 == 0:
        return value
    per = 8 // count
    found = value[0:count]
    for i in range(1, per):
        found = jnp.where(index % per == i, value[i * count : (i + 1) * count], found)
    return found


def place():
    return lax.axis_index("wide"), lax.axis_index("tail"), lax.axis_index("sub")


def pack_kernel(wide, cols, list_hbm, label_hbm, head_hbm, tail_hbm, core_hbm, *refs):
    z_refs, (x_ref, head_own, label_own, listed, label_ref, head_ref, sems) = refs[: wide - 1], refs[wide - 1 :]
    w, t, s = place()
    block, slots, width = label_ref.shape
    chunk = block // (2 * cols)
    rows = block // 2
    depth, half = tail_hbm.shape
    copies = [
        pltpu.make_async_copy(source, target, sems.at[i])
        for i, (source, target) in enumerate(
            (
                (list_hbm, listed),
                (label_hbm, label_ref),
                (head_hbm, head_ref),
                (tail_hbm, x_ref.at[0:depth]),
            )
        )
    ]
    for copy in copies:
        copy.start()
    copies[0].wait()
    count = jnp.int32(0)
    for j in range(slots):
        count = count + (listed[0, j] == w).astype(jnp.int32)
    x_ref[depth + rows :, :] = jnp.full((8, half), count.astype(F32), F32)
    label_own[block:, :] = jnp.full((8, width), count.astype(F32), F32)
    copies[1].wait()
    copies[2].wait()
    for part in range(2):
        for col in range(cols):
            start = pl.multiple_of((col * 2 + (s ^ part)) * chunk, chunk)
            at = part * rows + col * chunk
            embed = head_ref[pl.ds(start, chunk), :]
            head_own[at : at + chunk, :] = embed
            slot_labels = [label_ref[pl.ds(start, chunk), j, :] for j in range(slots)]
            for k in range(wide):
                total = jnp.zeros((chunk, width), jnp.int32)
                for j in range(slots):
                    total = total + jnp.where(listed[0, j] == (w ^ k), slot_labels[j], 0)
                total = total.astype(F32)
                if k == 0:
                    label_own[at : at + chunk, :] = total
                    lane = (at // rows) * width
                    row = depth + at % rows
                    x_ref[row : row + chunk, lane : lane + width] = total
                else:
                    z_refs[k - 1][at : at + chunk, half : half + width] = total
                    if part == 0:
                        z_refs[k - 1][at : at + chunk, 0:half] = embed[:, 0:half]
                        z_refs[k - 1][rows + at : rows + at + chunk, 0:half] = embed[:, half:]
    copies[3].wait()


def query_kernel(core_ref, core_other, *refs):
    tails, others, out_ref = refs[: len(refs) // 2], refs[len(refs) // 2 : -1], refs[-1]
    depth = tails[0].shape[0]
    total = None
    for core, parts in ((core_ref, tails), (core_other, others)):
        tail = jnp.concatenate([ref[0:depth, :] for ref in parts], axis=0)
        value = dot3(split(core[0]), split(tail), NT)
        total = value if total is None else total + value
    out_ref[...] = total


def grad_kernel(wide, cols, refs):
    (core_ref, core_other, query_ref, head_own, label_own, x_refs, z_refs, swap_refs, own_ref, joint_ref, fars,
     heads, resid, outer, turned) = refs
    w, t, s = place()
    block, dim = head_own.shape
    width = label_own.shape[1]
    rows = block // 2
    chunk = rows // cols
    half = core_ref.shape[2]
    heads[0:block, :] = head_own[...]
    for k in range(1, wide):
        at = k * block
        for part, ref in enumerate((z_refs[k - 1][0], swap_refs[k - 1][0])):
            heads[at + part * rows : at + part * rows + rows, 0:half] = ref[0:rows, 0:half]
            heads[at + part * rows : at + part * rows + rows, half:] = ref[rows:, 0:half]
    query = split(query_ref[...])
    head_parts = split(heads[...])
    score = dot3(head_parts, query, NN)
    prob = jax.nn.sigmoid(score)
    depth = x_refs[0].shape[0] - 8 - rows if x_refs else 0
    for o in range(cols):
        lanes = slice(o * width, (o + 1) * width)
        times = label_own[block : block + 1, :] if o == 0 else x_refs[o - 1][depth + rows : depth + rows + 1, 0:width]
        if o == 0:
            resid[0:block, lanes] = times * prob[0:block, lanes] - label_own[0:block, :]
        else:
            ref = x_refs[o - 1]
            for part in range(2):
                resid[part * rows : part * rows + rows, lanes] = (
                    times * prob[part * rows : part * rows + rows, lanes]
                    - ref[depth : depth + rows, part * width : (part + 1) * width]
                )
        for k in range(1, wide):
            first, last = (half, half + width) if o < 2 else (0, width)
            mine = z_refs[k - 1][o // 2][:, first:last]
            other = swap_refs[k - 1][o // 2]
            other = jnp.concatenate([other[rows:, first:last], other[0:rows, first:last]], axis=0)
            label = jnp.where(s == o % 2, mine, other)
            resid[k * block : (k + 1) * block, lanes] = times * prob[k * block : (k + 1) * block, lanes] - label
    resid_parts = split(resid[...])
    outer[...] = dot3(head_parts, resid_parts, TN)
    turned[...] = resid[...].T
    tail_rows = width // wide
    pitch = max(tail_rows, 8)
    asked = [w, w ^ 1] + [s * wide + (w ^ (2 * j + 1 - s)) for j in range(1, wide // 2)]
    mixed = dot3(split(jnp.concatenate([window(turned, index, tail_rows) for index in asked], axis=0)), head_parts, NN)
    tails = dot3(split(mixed), split(core_ref[0]), NN)
    tails_other = dot3(split(mixed[2 * pitch :]), split(core_other[0]), NN)
    starts = [k * block + t * chunk for k in range(2)]
    for j in range(1, wide // 2):
        starts += [(2 * j + 1 - s) * block + part * rows + (t ^ s) * chunk for part in range(2)]
    picked = [resid[pl.ds(pl.multiple_of(start, chunk), chunk), :] for start in starts]
    head_sum = dot3(split(jnp.concatenate(picked, axis=0)), query, NT)
    core_rows = dim // wide
    span = core_rows // 2

    def put_outer(ref, start, take, flip):
        piece = outer[pl.ds(pl.multiple_of(start, take), take), :]
        for i in range(cols // 2):
            first, last = piece[:, 2 * i * width : (2 * i + 1) * width], piece[:, (2 * i + 1) * width : 2 * (i + 1) * width]
            if flip:
                first, last = jnp.where(s == 0, first, last), jnp.where(s == 0, last, first)
            ref[i * take : (i + 1) * take, 0:width] = first
            ref[i * take : (i + 1) * take, width:] = last
        return cols // 2 * take

    def put_head(ref, at, item):
        for i in range(dim // half):
            ref[at : at + chunk, :] = head_sum[item * chunk : (item + 1) * chunk, i * half : (i + 1) * half]
            at += chunk
        return at

    for k, ref in enumerate((own_ref, joint_ref)):
        take = core_rows if k == 0 else span
        at = put_outer(ref, (w ^ k) * core_rows + (0 if k == 0 else s * span), take, False)
        at = put_head(ref, at, k)
        ref[at : at + tail_rows, :] = pick(tails[k * pitch : (k + 1) * pitch], w ^ k, tail_rows)
    for j, (outer_ref, sum_ref) in enumerate(fars, 1):
        target = w ^ (2 * j + 1 - s)
        put_outer(outer_ref, target * core_rows, core_rows, True)
        at = put_head(sum_ref, put_head(sum_ref, 0, 2 * j), 2 * j + 1)
        for values, first in ((tails, (j + 1) * pitch), (tails_other, (j - 1) * pitch)):
            sum_ref[at : at + tail_rows, :] = pick(values[first : first + pitch], target, tail_rows)
            at += pitch


def finish_kernel(wide, cols, scales, tail_ref, x_refs, own_ref, joint, fars, head_out, tail_out, core_out, pieces):
    w, t, s = place()
    depth, half = tail_ref.shape
    core_rows = core_out.shape[1]
    span = core_rows // 2
    chunk, dim = head_out.shape
    tail_rows = tail_out.shape[1]
    chunks = cols * depth // half
    each = wide // cols

    def keep(relation, parts):
        @pl.when(relation // each == t)
        def _():
            at = relation % each
            for ref, start, take in parts:
                for i in range(chunks):
                    pieces[at, pl.ds(pl.multiple_of(start, take), take), i * half : (i + 1) * half] = (
                        ref[i * take : (i + 1) * take, :]
                    )

    keep(w, [(own_ref, 0, core_rows)])
    keep(w ^ 1, [(joint[0], s * span, span), (joint[1], (1 - s) * span, span)])
    lead = [(own_ref, chunks * core_rows, 0), (joint[0], chunks * span, 0)]
    for j, (outer_in, outer_swap, sum_in, sum_swap) in enumerate(fars, 1):
        keep(w ^ (2 * j + 1 - s), [(outer_in, 0, core_rows)])
        keep(w ^ (2 * j + s), [(outer_swap, 0, core_rows)])
        lead += [(sum_in, 0, 0), (sum_swap, 0, 1)]
    heads = dim // half * chunk
    pitch = -(-tail_rows // 8) * 8
    for i in range(dim // half):
        total = sum(ref[at + part * heads + i * chunk : at + part * heads + (i + 1) * chunk, :] for ref, at, part in lead)
        head_out[:, i * half : (i + 1) * half] = total * scales[0]
    total = 0.0
    for n, (ref, at, part) in enumerate(lead):
        at += heads if n < 2 else 2 * heads + part * pitch
        total = total + ref[at : at + tail_rows, :]
    tail_out[0] = total * scales[1]
    tails = split(jnp.concatenate([tail_ref[...]] + [x[0:depth, :] for x in x_refs], axis=0))
    for i in range(each):
        core_out[i] = dot3(split(pieces[i]), tails, NN) * scales[2]


def call(kernel, inputs, outputs, scratch=(), hbm=(), flops=0, limit=VMEM_LIMIT):
    vmem, far = pl.BlockSpec(memory_space=pltpu.VMEM), pl.BlockSpec(memory_space=pltpu.HBM)
    return pl.pallas_call(
        kernel,
        out_shape=tuple(jax.ShapeDtypeStruct(shape, F32) for shape in outputs),
        in_specs=[far if i in hbm else vmem for i in range(len(inputs))],
        out_specs=tuple(vmem for _ in outputs),
        scratch_shapes=[pltpu.VMEM(item, F32) if isinstance(item, tuple) else item for item in scratch],
        compiler_params=pltpu.CompilerParams(vmem_limit_bytes=limit),
        cost_estimate=pl.CostEstimate(flops=flops, bytes_accessed=4 * sum(x.size for x in inputs), transcendentals=0),
    )(*inputs)


def body(head_embed, tail_embed, core_mats, labels, core_lists):
    wide, cols = lax.axis_size("wide"), lax.axis_size("tail")
    block, dim = head_embed.shape
    depth, half = tail_embed.shape
    slots = core_lists.shape[1]
    rows = block // 2
    chunk = rows // cols
    axes = ("wide", "tail", "sub")

    def move(value, k, offsets=(0, 0), flip=0, owners=False):
        steps = k if isinstance(k, tuple) else (k, k)
        pairs = []
        for w in range(wide):
            for t in range(cols):
                for s in range(2):
                    line = t ^ offsets[s]
                    if not owners or line == w // (wide // cols):
                        target = ((w ^ steps[s]) * cols + line) * 2 + (s ^ flip)
                        pairs.append(((w * cols + t) * 2 + s, target))
        return lax.ppermute(value, axes, pairs)

    core_other = move(core_mats, 0, flip=1)
    order = [wide - 1] + list(range(1, wide - 1))
    packed = call(
        functools.partial(pack_kernel, wide, cols),
        (core_lists, labels, head_embed, tail_embed, core_mats),
        [(block, half + depth)] * (wide - 1)
        + [(depth + rows + 8, half), (block, dim), (block + 8, depth)],
        scratch=[
            pltpu.SMEM(core_lists.shape, jnp.int32),
            pltpu.VMEM(labels.shape, jnp.int32),
            head_embed.shape,
            pltpu.SemaphoreType.DMA((4,)),
        ],
        hbm=range(5),
        limit=FULL_LIMIT,
    )
    z_out, (x_out, head_own, label_own) = packed[: wide - 1], packed[wide - 1 :]
    z_in, z_swap = {}, {}
    for k in order:
        got = []
        for j in range(max(1, cols // 2)):
            sent = z_out[k - 1] if j == 0 else z_out[k - 1][:, half:]
            got.append(move(sent, k, (2 * j, (2 * j + 1) % cols)))
        z_in[k] = got
    x_in = [move(x_out, 0, (o, o)) for o in range(1, cols)]
    tail_other = move(lax.optimization_barrier((tail_embed, core_other))[0], 0, flip=1)
    ready = lax.optimization_barrier((x_in, z_in[order[0]]))[0]
    x_other = [move(value, 0, flip=1) for value in ready]
    (query,) = call(
        query_kernel,
        (core_mats, core_other, tail_embed, *x_in, tail_other, *x_other),
        [(dim, cols * depth)],
    )
    for k in order:
        ready = z_in[k]
        z_swap[k] = [move(value, 0, flip=1) for value in ready]

    per = len(z_in[1])
    flat_in = [value for k in order for value in z_in[k]]
    flat_swap = [value for k in order for value in z_swap[k]]
    core_rows, tail_rows = dim // wide, depth // wide
    chunks = cols * depth // half
    small = dim // half * chunk + -(-tail_rows // 8) * 8
    own_shape = (chunks * core_rows + small, half)
    joint_shape = (chunks * core_rows // 2 + small, half)
    pairs = range(1, wide // 2)

    def grads(core_ref, other_ref, query_ref, head_ref, label_ref, *rest):
        x_refs, rest = rest[: cols - 1], rest[cols - 1 :]
        count = len(flat_in)
        group = lambda refs: [refs[order.index(k) * per : order.index(k) * per + per] for k in range(1, wide)]
        z_refs, swap_refs, rest = group(rest[:count]), group(rest[count : 2 * count]), rest[2 * count :]
        own_ref, joint_ref, rest = rest[0], rest[1], rest[2:]
        fars, scratch = list(zip(rest[0 : 2 * len(pairs) : 2], rest[1 : 2 * len(pairs) : 2])), rest[2 * len(pairs) :]
        grad_kernel(
            wide, cols,
            (core_ref, other_ref, query_ref, head_ref, label_ref, x_refs, z_refs, swap_refs, own_ref, joint_ref, fars)
            + tuple(scratch),
        )

    made = call(
        grads,
        (core_mats, core_other, query, head_own, label_own, *x_in, *flat_in, *flat_swap),
        [own_shape, joint_shape] + [(chunks * core_rows, half), (2 * small, half)] * len(pairs),
        scratch=[
            (wide * block, dim), (wide * block, cols * depth), (dim, cols * depth), (cols * depth, wide * block),
        ],
        flops=6 * wide * block * dim * cols * depth * 2,
    )
    own, far = made[0], []
    for j in pairs:
        steps = (2 * j + 1, 2 * j)
        far.append([move(made[2 * j], steps, (0, 1), owners=True), move(made[2 * j + 1], steps, (0, 1))])
    joint = move(made[1], 1)
    far = [(a, move(a, 0, flip=1), b, move(b, 0, flip=1)) for a, b in far]
    joint_swap = move(joint, 0, flip=1)
    heads_total, tails_total = block * wide, depth * cols
    scales = (
        1.0 / math.sqrt(slots * tails_total),
        1.0 / math.sqrt(slots * heads_total),
        1.0 / math.sqrt(heads_total * depth),
    )
    each = wide // cols

    def finish(tail_ref, *rest):
        x_refs, rest = rest[: cols - 1], rest[cols - 1 :]
        own_ref, rest = rest[0], rest[1:]
        far_s, rest = rest[: 2 * len(pairs)], rest[2 * len(pairs) :]
        joint_refs, rest = rest[:2], rest[2:]
        far_u, rest = rest[: 2 * len(pairs)], rest[2 * len(pairs) :]
        fars = [far_u[2 * i : 2 * i + 2] + far_s[2 * i : 2 * i + 2] for i in range(len(pairs))]
        finish_kernel(wide, cols, scales, tail_ref, x_refs, own_ref, joint_refs, fars, *rest)

    return call(
        finish,
        (tail_embed, *x_in, own, *[v for g in far for v in g[2:]], joint, joint_swap, *[v for g in far for v in g[:2]]),
        [(chunk, dim), (1, tail_rows, half), (each, core_rows, half)],
        scratch=[(each, core_rows, cols * depth)],
        flops=6 * each * core_rows * cols * depth * half,
    )


def solution(mesh):
    in_specs = (
        P(("groups", "wide"), None),
        P(("groups", "tail"), "sub"),
        P(("groups", "wide"), None, "sub"),
        P(("groups", "wide"), None, "tail"),
        P(("groups", "tail"), None),
    )
    out_specs = (
        P(("groups", "wide", "tail", "sub"), None),
        P(("groups", "tail"), "wide", "sub"),
        P(("groups", "tail"), "wide", "sub"),
    )
    return jax.shard_map(body, mesh=mesh, in_specs=in_specs, out_specs=out_specs, check_vma=False)
```

```python
import functools
import math

import jax
import jax.numpy as jnp
from jax import lax
from jax.experimental import pallas as pl
from jax.experimental.pallas import tpu as pltpu
from jax.sharding import PartitionSpec as P


F32 = jnp.float32
VMEM_LIMIT = 48 * 1024 * 1024
FULL_LIMIT = 62 * 1024 * 1024
NN = (((1,), (0,)), ((), ()))
NT = (((1,), (1,)), ((), ()))
TN = (((0,), (0,)), ((), ()))


def split(value):
    high = value.astype(jnp.bfloat16)
    low = (value - high.astype(F32)).astype(jnp.bfloat16)
    return high, low


def dot3(left, right, dims):
    lh, ll = left
    rh, rl = right
    mul = functools.partial(lax.dot_general, dimension_numbers=dims, preferred_element_type=F32)
    free = 1 - dims[0][0][0]
    size = lh.shape[free]
    both = mul(jnp.concatenate([lh, ll], axis=free), rh)
    return both[:size] + (mul(lh, rl) + both[size:])


def window(ref, index, count):
    size = max(count, 8)
    return ref[pl.ds(pl.multiple_of(index * count // size * size, size), size), :]


def pick(value, index, count):
    if count % 8 == 0:
        return value
    per = 8 // count
    found = value[0:count]
    for i in range(1, per):
        found = jnp.where(index % per == i, value[i * count : (i + 1) * count], found)
    return found


def place():
    return lax.axis_index("wide"), lax.axis_index("tail"), lax.axis_index("sub")


def pack_kernel(wide, cols, list_hbm, label_hbm, head_hbm, tail_hbm, core_hbm, *refs):
    z_refs, (x_ref, head_own, label_own, listed, label_ref, head_ref, sems) = refs[: wide - 1], refs[wide - 1 :]
    w, t, s = place()
    block, slots, width = label_ref.shape
    chunk = block // (2 * cols)
    rows = block // 2
    depth, half = tail_hbm.shape
    copies = [
        pltpu.make_async_copy(source, target, sems.at[i])
        for i, (source, target) in enumerate(
            (
                (list_hbm, listed),
                (label_hbm, label_ref),
                (head_hbm, head_ref),
                (tail_hbm, x_ref.at[0:depth]),
            )
        )
    ]
    for copy in copies:
        copy.start()
    copies[0].wait()
    count = jnp.int32(0)
    for j in range(slots):
        count = count + (listed[0, j] == w).astype(jnp.int32)
    x_ref[depth + rows :, :] = jnp.full((8, half), count.astype(F32), F32)
    label_own[block:, :] = jnp.full((8, width), count.astype(F32), F32)
    copies[1].wait()
    copies[2].wait()
    for part in range(2):
        for col in range(cols):
            start = pl.multiple_of((col * 2 + (s ^ part)) * chunk, chunk)
            at = part * rows + col * chunk
            embed = head_ref[pl.ds(start, chunk), :]
            head_own[at : at + chunk, :] = embed
            slot_labels = [label_ref[pl.ds(start, chunk), j, :] for j in range(slots)]
            for k in range(wide):
                total = jnp.zeros((chunk, width), jnp.int32)
                for j in range(slots):
                    total = total + jnp.where(listed[0, j] == (w ^ k), slot_labels[j], 0)
                total = total.astype(F32)
                if k == 0:
                    label_own[at : at + chunk, :] = total
                    lane = (at // rows) * width
                    row = depth + at % rows
                    x_ref[row : row + chunk, lane : lane + width] = total
                else:
                    z_refs[k - 1][at : at + chunk, half : half + width] = total
                    if part == 0:
                        z_refs[k - 1][at : at + chunk, 0:half] = embed[:, 0:half]
                        z_refs[k - 1][rows + at : rows + at + chunk, 0:half] = embed[:, half:]
    copies[3].wait()


def query_kernel(core_ref, core_other, *refs):
    others, tails, out_ref = refs[: len(refs) // 2], refs[len(refs) // 2 : -1], refs[-1]
    depth = tails[0].shape[0]
    total = None
    for core, parts in ((core_ref, tails), (core_other, others)):
        tail = jnp.concatenate([ref[0:depth, :] for ref in parts], axis=0)
        value = dot3(split(core[0]), split(tail), NT)
        total = value if total is None else total + value
    out_ref[...] = total


def grad_kernel(wide, cols, refs):
    (core_ref, core_other, query_ref, head_own, label_own, x_refs, z_refs, swap_refs, own_ref, joint_ref, fars,
     heads, resid, outer, turned) = refs
    w, t, s = place()
    block, dim = head_own.shape
    width = label_own.shape[1]
    rows = block // 2
    chunk = rows // cols
    half = core_ref.shape[2]
    heads[0:block, :] = head_own[...]
    for k in range(1, wide):
        at = k * block
        for part, ref in enumerate((z_refs[k - 1][0], swap_refs[k - 1][0])):
            heads[at + part * rows : at + part * rows + rows, 0:half] = ref[0:rows, 0:half]
            heads[at + part * rows : at + part * rows + rows, half:] = ref[rows:, 0:half]
    query = split(query_ref[...])
    head_parts = split(heads[...])
    score = dot3(head_parts, query, NN)
    prob = jax.nn.sigmoid(score)
    depth = x_refs[0].shape[0] - 8 - rows if x_refs else 0
    for o in range(cols):
        lanes = slice(o * width, (o + 1) * width)
        times = label_own[block : block + 1, :] if o == 0 else x_refs[o - 1][depth + rows : depth + rows + 1, 0:width]
        if o == 0:
            resid[0:block, lanes] = times * prob[0:block, lanes] - label_own[0:block, :]
        else:
            ref = x_refs[o - 1]
            for part in range(2):
                resid[part * rows : part * rows + rows, lanes] = (
                    times * prob[part * rows : part * rows + rows, lanes]
                    - ref[depth : depth + rows, part * width : (part + 1) * width]
                )
        for k in range(1, wide):
            first, last = (half, half + width) if o < 2 else (0, width)
            mine = z_refs[k - 1][o // 2][:, first:last]
            other = swap_refs[k - 1][o // 2]
            other = jnp.concatenate([other[rows:, first:last], other[0:rows, first:last]], axis=0)
            label = jnp.where(s == o % 2, mine, other)
            resid[k * block : (k + 1) * block, lanes] = times * prob[k * block : (k + 1) * block, lanes] - label
    resid_parts = split(resid[...])
    starts = [k * block + t * chunk for k in range(2)]
    for j in range(1, wide // 2):
        starts += [(2 * j + 1 - s) * block + part * rows + (t ^ s) * chunk for part in range(2)]
    picked = [resid[pl.ds(pl.multiple_of(start, chunk), chunk), :] for start in starts]
    head_sum = dot3(split(jnp.concatenate(picked, axis=0)), query, NT)
    outer[...] = dot3(head_parts, resid_parts, TN)
    turned[...] = resid[...].T
    tail_rows = width // wide
    pitch = max(tail_rows, 8)
    asked = [w, w ^ 1] + [s * wide + (w ^ (2 * j + 1 - s)) for j in range(1, wide // 2)]
    mixed = dot3(split(jnp.concatenate([window(turned, index, tail_rows) for index in asked], axis=0)), head_parts, NN)
    tails = dot3(split(mixed), split(core_ref[0]), NN)
    tails_other = dot3(split(mixed[2 * pitch :]), split(core_other[0]), NN)
    core_rows = dim // wide
    span = core_rows // 2

    def put_outer(ref, start, take, flip):
        piece = outer[pl.ds(pl.multiple_of(start, take), take), :]
        for i in range(cols // 2):
            first, last = piece[:, 2 * i * width : (2 * i + 1) * width], piece[:, (2 * i + 1) * width : 2 * (i + 1) * width]
            if flip:
                first, last = jnp.where(s == 0, first, last), jnp.where(s == 0, last, first)
            ref[i * take : (i + 1) * take, 0:width] = first
            ref[i * take : (i + 1) * take, width:] = last
        return cols // 2 * take

    def put_head(ref, at, item):
        for i in range(dim // half):
            ref[at : at + chunk, :] = head_sum[item * chunk : (item + 1) * chunk, i * half : (i + 1) * half]
            at += chunk
        return at

    for k, ref in enumerate((own_ref, joint_ref)):
        take = core_rows if k == 0 else span
        at = put_outer(ref, (w ^ k) * core_rows + (0 if k == 0 else s * span), take, False)
        at = put_head(ref, at, k)
        ref[at : at + tail_rows, :] = pick(tails[k * pitch : (k + 1) * pitch], w ^ k, tail_rows)
    for j, (outer_ref, sum_ref) in enumerate(fars, 1):
        target = w ^ (2 * j + 1 - s)
        put_outer(outer_ref, target * core_rows, core_rows, True)
        at = put_head(sum_ref, put_head(sum_ref, 0, 2 * j), 2 * j + 1)
        for values, first in ((tails, (j + 1) * pitch), (tails_other, (j - 1) * pitch)):
            sum_ref[at : at + tail_rows, :] = pick(values[first : first + pitch], target, tail_rows)
            at += pitch


def finish_kernel(wide, cols, scales, tail_ref, x_refs, own_ref, joint, fars, head_out, tail_out, core_out, pieces):
    w, t, s = place()
    depth, half = tail_ref.shape
    core_rows = core_out.shape[1]
    span = core_rows // 2
    chunk, dim = head_out.shape
    tail_rows = tail_out.shape[1]
    chunks = cols * depth // half
    each = wide // cols

    def keep(relation, parts):
        @pl.when(relation // each == t)
        def _():
            at = relation % each
            for ref, start, take in parts:
                for i in range(chunks):
                    pieces[at, pl.ds(pl.multiple_of(start, take), take), i * half : (i + 1) * half] = (
                        ref[i * take : (i + 1) * take, :]
                    )

    keep(w, [(own_ref, 0, core_rows)])
    keep(w ^ 1, [(joint[0], s * span, span), (joint[1], (1 - s) * span, span)])
    lead = [(own_ref, chunks * core_rows, 0), (joint[0], chunks * span, 0)]
    for j, (outer_in, outer_swap, sum_in, sum_swap) in enumerate(fars, 1):
        keep(w ^ (2 * j + 1 - s), [(outer_in, 0, core_rows)])
        keep(w ^ (2 * j + s), [(outer_swap, 0, core_rows)])
        lead += [(sum_in, 0, 0), (sum_swap, 0, 1)]
    heads = dim // half * chunk
    pitch = -(-tail_rows // 8) * 8
    for i in range(dim // half):
        total = sum(ref[at + part * heads + i * chunk : at + part * heads + (i + 1) * chunk, :] for ref, at, part in lead)
        head_out[:, i * half : (i + 1) * half] = total * scales[0]
    total = 0.0
    for n, (ref, at, part) in enumerate(lead):
        at += heads if n < 2 else 2 * heads + part * pitch
        total = total + ref[at : at + tail_rows, :]
    tail_out[0] = total * scales[1]
    tails = split(jnp.concatenate([tail_ref[...]] + [x[0:depth, :] for x in x_refs], axis=0))
    whole = pieces[...].reshape(each * core_rows, cols * depth)
    core_out[...] = (dot3(split(whole), tails, NN) * scales[2]).reshape(each, core_rows, half)


def call(kernel, inputs, outputs, scratch=(), hbm=(), flops=0, limit=VMEM_LIMIT, traffic=None):
    vmem, far = pl.BlockSpec(memory_space=pltpu.VMEM), pl.BlockSpec(memory_space=pltpu.HBM)
    return pl.pallas_call(
        kernel,
        out_shape=tuple(jax.ShapeDtypeStruct(shape, F32) for shape in outputs),
        in_specs=[far if i in hbm else vmem for i in range(len(inputs))],
        out_specs=tuple(vmem for _ in outputs),
        scratch_shapes=[pltpu.VMEM(item, F32) if isinstance(item, tuple) else item for item in scratch],
        compiler_params=pltpu.CompilerParams(vmem_limit_bytes=limit),
        cost_estimate=pl.CostEstimate(flops=flops, bytes_accessed=4 * sum(x.size for x in inputs) if traffic is None else traffic, transcendentals=0),
    )(*inputs)


def body(head_embed, tail_embed, core_mats, labels, core_lists):
    wide, cols = lax.axis_size("wide"), lax.axis_size("tail")
    block, dim = head_embed.shape
    depth, half = tail_embed.shape
    slots = core_lists.shape[1]
    rows = block // 2
    chunk = rows // cols
    axes = ("wide", "tail", "sub")

    def move(value, k, offsets=(0, 0), flip=0, owners=False):
        steps = k if isinstance(k, tuple) else (k, k)
        pairs = []
        for w in range(wide):
            for t in range(cols):
                for s in range(2):
                    line = t ^ offsets[s]
                    if not owners or line == w // (wide // cols):
                        target = ((w ^ steps[s]) * cols + line) * 2 + (s ^ flip)
                        pairs.append(((w * cols + t) * 2 + s, target))
        return lax.ppermute(value, axes, pairs)

    core_other = move(core_mats, 0, flip=1)
    order = [wide - 1] + list(range(1, wide - 1))
    packed = call(
        functools.partial(pack_kernel, wide, cols),
        (core_lists, labels, head_embed, tail_embed, core_mats),
        [(block, half + depth)] * (wide - 1)
        + [(depth + rows + 8, half), (block, dim), (block + 8, depth)],
        scratch=[
            pltpu.SMEM(core_lists.shape, jnp.int32),
            pltpu.VMEM(labels.shape, jnp.int32),
            head_embed.shape,
            pltpu.SemaphoreType.DMA((4,)),
        ],
        hbm=range(5),
        limit=FULL_LIMIT,
    )
    z_out, (x_out, head_own, label_own) = packed[: wide - 1], packed[wide - 1 :]
    z_in, z_swap = {}, {}
    for k in order:
        got = []
        for j in range(max(1, cols // 2)):
            sent = z_out[k - 1] if j == 0 else z_out[k - 1][:, half:]
            got.append(move(sent, k, (2 * j, (2 * j + 1) % cols)))
        z_in[k] = got
    x_in = [move(x_out, 0, (o, o)) for o in range(1, cols)]
    tail_other = move(lax.optimization_barrier((tail_embed, core_other))[0], 0, flip=1)
    ready = lax.optimization_barrier((x_in, z_in[order[0]]))[0]
    x_other = [move(value, 0, flip=1) for value in ready]
    (query,) = call(
        query_kernel,
        (core_mats, core_other, tail_other, *x_other, tail_embed, *x_in),
        [(dim, cols * depth)],
        traffic=0,
    )
    for k in order:
        ready = z_in[k]
        z_swap[k] = [move(value, 0, flip=1) for value in ready]

    per = len(z_in[1])
    flat_in = [value for k in order for value in z_in[k]]
    flat_swap = [value for k in order for value in z_swap[k]]
    core_rows, tail_rows = dim // wide, depth // wide
    chunks = cols * depth // half
    small = dim // half * chunk + -(-tail_rows // 8) * 8
    own_shape = (chunks * core_rows + small, half)
    joint_shape = (chunks * core_rows // 2 + small, half)
    pairs = range(1, wide // 2)

    def grads(core_ref, other_ref, query_ref, head_ref, label_ref, *rest):
        x_refs, rest = rest[: cols - 1], rest[cols - 1 :]
        count = len(flat_in)
        group = lambda refs: [refs[order.index(k) * per : order.index(k) * per + per] for k in range(1, wide)]
        z_refs, swap_refs, rest = group(rest[:count]), group(rest[count : 2 * count]), rest[2 * count :]
        own_ref, joint_ref, rest = rest[0], rest[1], rest[2:]
        fars, scratch = list(zip(rest[0 : 2 * len(pairs) : 2], rest[1 : 2 * len(pairs) : 2])), rest[2 * len(pairs) :]
        grad_kernel(
            wide, cols,
            (core_ref, other_ref, query_ref, head_ref, label_ref, x_refs, z_refs, swap_refs, own_ref, joint_ref, fars)
            + tuple(scratch),
        )

    made = call(
        grads,
        (core_mats, core_other, query, head_own, label_own, *x_in, *flat_in, *flat_swap),
        [own_shape, joint_shape] + [(chunks * core_rows, half), (2 * small, half)] * len(pairs),
        scratch=[
            (wide * block, dim), (wide * block, cols * depth), (dim, cols * depth), (cols * depth, wide * block),
        ],
        flops=6 * wide * block * dim * cols * depth * 2,
    )
    own, far = made[0], []
    for j in pairs:
        steps = (2 * j + 1, 2 * j)
        far.append([move(made[2 * j], steps, (0, 1), owners=True), move(made[2 * j + 1], steps, (0, 1))])
    joint = move(made[1], 1)
    far = [(a, move(a, 0, flip=1), b, move(b, 0, flip=1)) for a, b in far]
    joint_swap = move(joint, 0, flip=1)
    heads_total, tails_total = block * wide, depth * cols
    scales = (
        1.0 / math.sqrt(slots * tails_total),
        1.0 / math.sqrt(slots * heads_total),
        1.0 / math.sqrt(heads_total * depth),
    )
    each = wide // cols

    def finish(own_ref, *rest):
        far_s, rest = rest[: 2 * len(pairs)], rest[2 * len(pairs) :]
        joint_refs, rest = rest[:2], rest[2:]
        far_u, rest = rest[: 2 * len(pairs)], rest[2 * len(pairs) :]
        tail_ref, x_refs, rest = rest[0], rest[1:cols], rest[cols:]
        fars = [far_u[2 * i : 2 * i + 2] + far_s[2 * i : 2 * i + 2] for i in range(len(pairs))]
        finish_kernel(wide, cols, scales, tail_ref, x_refs, own_ref, joint_refs, fars, *rest)

    return call(
        finish,
        (own, *[v for g in far for v in g[2:]], joint, joint_swap, *[v for g in far for v in g[:2]], tail_embed, *x_in),
        [(chunk, dim), (1, tail_rows, half), (each, core_rows, half)],
        scratch=[(each, core_rows, cols * depth)],
        flops=6 * each * core_rows * cols * depth * half,
    )


def solution(mesh):
    in_specs = (
        P(("groups", "wide"), None),
        P(("groups", "tail"), "sub"),
        P(("groups", "wide"), None, "sub"),
        P(("groups", "wide"), None, "tail"),
        P(("groups", "tail"), None),
    )
    out_specs = (
        P(("groups", "wide", "tail", "sub"), None),
        P(("groups", "tail"), "wide", "sub"),
        P(("groups", "tail"), "wide", "sub"),
    )
    return jax.shard_map(body, mesh=mesh, in_specs=in_specs, out_specs=out_specs, check_vma=False)
```

```python
import functools
import math

import jax
import jax.numpy as jnp
from jax import lax
from jax.experimental import pallas as pl
from jax.experimental.pallas import tpu as pltpu
from jax.sharding import PartitionSpec as P


F32 = jnp.float32
VMEM_LIMIT = 48 * 1024 * 1024
FULL_LIMIT = 62 * 1024 * 1024
NN = (((1,), (0,)), ((), ()))
NT = (((1,), (1,)), ((), ()))
TN = (((0,), (0,)), ((), ()))


def split(value):
    high = value.astype(jnp.bfloat16)
    low = (value - high.astype(F32)).astype(jnp.bfloat16)
    return high, low


def dot3(left, right, dims):
    lh, ll = left
    rh, rl = right
    mul = functools.partial(lax.dot_general, dimension_numbers=dims, preferred_element_type=F32)
    free = 1 - dims[0][0][0]
    size = lh.shape[free]
    both = mul(jnp.concatenate([lh, ll], axis=free), rh)
    return both[:size] + (mul(lh, rl) + both[size:])


def window(ref, index, count):
    size = max(count, 8)
    return ref[pl.ds(pl.multiple_of(index * count // size * size, size), size), :]


def pick(value, index, count):
    if count % 8 == 0:
        return value
    per = 8 // count
    found = value[0:count]
    for i in range(1, per):
        found = jnp.where(index % per == i, value[i * count : (i + 1) * count], found)
    return found


def place():
    return lax.axis_index("wide"), lax.axis_index("tail"), lax.axis_index("sub")


def pack_kernel(wide, cols, list_hbm, label_hbm, head_hbm, tail_hbm, core_hbm, *refs):
    z_refs, (x_ref, label_own, listed, label_ref, head_ref, sems) = refs[: wide - 1], refs[wide - 1 :]
    w, t, s = place()
    block, slots, width = label_ref.shape
    chunk = block // (2 * cols)
    rows = block // 2
    depth, half = tail_hbm.shape
    copies = [
        pltpu.make_async_copy(source, target, sems.at[i])
        for i, (source, target) in enumerate(
            (
                (list_hbm, listed),
                (label_hbm, label_ref),
                (head_hbm, head_ref),
                (tail_hbm, x_ref.at[0:depth]),
            )
        )
    ]
    for copy in copies:
        copy.start()
    copies[0].wait()
    count = jnp.int32(0)
    for j in range(slots):
        count = count + (listed[0, j] == w).astype(jnp.int32)
    x_ref[depth + rows :, :] = jnp.full((8, half), count.astype(F32), F32)
    label_own[block:, :] = jnp.full((8, width), count.astype(F32), F32)
    copies[1].wait()
    copies[2].wait()
    for part in range(2):
        for col in range(cols):
            start = pl.multiple_of((col * 2 + (s ^ part)) * chunk, chunk)
            at = part * rows + col * chunk
            embed = head_ref[pl.ds(start, chunk), :]
            slot_labels = [label_ref[pl.ds(start, chunk), j, :] for j in range(slots)]
            for k in range(wide):
                total = jnp.zeros((chunk, width), jnp.int32)
                for j in range(slots):
                    total = total + jnp.where(listed[0, j] == (w ^ k), slot_labels[j], 0)
                total = total.astype(F32)
                if k == 0:
                    label_own[at : at + chunk, :] = total
                    lane = (at // rows) * width
                    row = depth + at % rows
                    x_ref[row : row + chunk, lane : lane + width] = total
                else:
                    z_refs[k - 1][at : at + chunk, half : half + width] = total
                    if part == 0:
                        z_refs[k - 1][at : at + chunk, 0:half] = embed[:, 0:half]
                        z_refs[k - 1][rows + at : rows + at + chunk, 0:half] = embed[:, half:]
    copies[3].wait()


def query_kernel(core_ref, core_other, *refs):
    others, tails, out_ref = refs[: len(refs) // 2], refs[len(refs) // 2 : -1], refs[-1]
    depth = tails[0].shape[0]
    total = None
    for core, parts in ((core_ref, tails), (core_other, others)):
        tail = jnp.concatenate([ref[0:depth, :] for ref in parts], axis=0)
        value = dot3(split(core[0]), split(tail), NT)
        total = value if total is None else total + value
    out_ref[...] = total


def grad_kernel(wide, cols, refs):
    (core_ref, core_other, query_ref, head_own, label_own, x_refs, z_refs, swap_refs, own_ref, joint_ref, fars,
     heads, resid, outer, turned) = refs
    w, t, s = place()
    block, dim = head_own.shape
    width = label_own.shape[1]
    rows = block // 2
    chunk = rows // cols
    half = core_ref.shape[2]
    for i in range(2 * cols):
        part, col = divmod(i, cols)
        start = pl.multiple_of((col * 2 + (s ^ part)) * chunk, chunk)
        heads[i * chunk : (i + 1) * chunk, :] = head_own[pl.ds(start, chunk), :]
    for k in range(1, wide):
        at = k * block
        for part, ref in enumerate((z_refs[k - 1][0], swap_refs[k - 1][0])):
            heads[at + part * rows : at + part * rows + rows, 0:half] = ref[0:rows, 0:half]
            heads[at + part * rows : at + part * rows + rows, half:] = ref[rows:, 0:half]
    query = split(query_ref[...])
    head_parts = split(heads[...])
    score = dot3(head_parts, query, NN)
    prob = jax.nn.sigmoid(score)
    depth = x_refs[0].shape[0] - 8 - rows if x_refs else 0
    for o in range(cols):
        lanes = slice(o * width, (o + 1) * width)
        times = label_own[block : block + 1, :] if o == 0 else x_refs[o - 1][depth + rows : depth + rows + 1, 0:width]
        if o == 0:
            resid[0:block, lanes] = times * prob[0:block, lanes] - label_own[0:block, :]
        else:
            ref = x_refs[o - 1]
            for part in range(2):
                resid[part * rows : part * rows + rows, lanes] = (
                    times * prob[part * rows : part * rows + rows, lanes]
                    - ref[depth : depth + rows, part * width : (part + 1) * width]
                )
        for k in range(1, wide):
            first, last = (half, half + width) if o < 2 else (0, width)
            mine = z_refs[k - 1][o // 2][:, first:last]
            other = swap_refs[k - 1][o // 2]
            other = jnp.concatenate([other[rows:, first:last], other[0:rows, first:last]], axis=0)
            label = jnp.where(s == o % 2, mine, other)
            resid[k * block : (k + 1) * block, lanes] = times * prob[k * block : (k + 1) * block, lanes] - label
    resid_parts = split(resid[...])
    starts = [k * block + t * chunk for k in range(2)]
    for j in range(1, wide // 2):
        starts += [(2 * j + 1 - s) * block + part * rows + (t ^ s) * chunk for part in range(2)]
    picked = [resid[pl.ds(pl.multiple_of(start, chunk), chunk), :] for start in starts]
    head_sum = dot3(split(jnp.concatenate(picked, axis=0)), query, NT)
    outer[...] = dot3(head_parts, resid_parts, TN)
    turned[...] = resid[...].T
    tail_rows = width // wide
    pitch = max(tail_rows, 8)
    asked = [w, w ^ 1] + [s * wide + (w ^ (2 * j + 1 - s)) for j in range(1, wide // 2)]
    mixed = dot3(split(jnp.concatenate([window(turned, index, tail_rows) for index in asked], axis=0)), head_parts, NN)
    tails = dot3(split(mixed), split(core_ref[0]), NN)
    tails_other = dot3(split(mixed[2 * pitch :]), split(core_other[0]), NN)
    core_rows = dim // wide
    span = core_rows // 2

    def put_outer(ref, start, take, flip):
        piece = outer[pl.ds(pl.multiple_of(start, take), take), :]
        for i in range(cols // 2):
            first, last = piece[:, 2 * i * width : (2 * i + 1) * width], piece[:, (2 * i + 1) * width : 2 * (i + 1) * width]
            if flip:
                first, last = jnp.where(s == 0, first, last), jnp.where(s == 0, last, first)
            ref[i * take : (i + 1) * take, 0:width] = first
            ref[i * take : (i + 1) * take, width:] = last
        return cols // 2 * take

    def put_head(ref, at, item):
        for i in range(dim // half):
            ref[at : at + chunk, :] = head_sum[item * chunk : (item + 1) * chunk, i * half : (i + 1) * half]
            at += chunk
        return at

    for k, ref in enumerate((own_ref, joint_ref)):
        take = core_rows if k == 0 else span
        at = put_outer(ref, (w ^ k) * core_rows + (0 if k == 0 else s * span), take, False)
        at = put_head(ref, at, k)
        ref[at : at + tail_rows, :] = pick(tails[k * pitch : (k + 1) * pitch], w ^ k, tail_rows)
    for j, (outer_ref, sum_ref) in enumerate(fars, 1):
        target = w ^ (2 * j + 1 - s)
        put_outer(outer_ref, target * core_rows, core_rows, True)
        at = put_head(sum_ref, put_head(sum_ref, 0, 2 * j), 2 * j + 1)
        for values, first in ((tails, (j + 1) * pitch), (tails_other, (j - 1) * pitch)):
            sum_ref[at : at + tail_rows, :] = pick(values[first : first + pitch], target, tail_rows)
            at += pitch


def finish_kernel(wide, cols, scales, tail_ref, x_refs, own_ref, joint, fars, head_out, tail_out, core_out, pieces):
    w, t, s = place()
    depth, half = tail_ref.shape
    core_rows = core_out.shape[1]
    span = core_rows // 2
    chunk, dim = head_out.shape
    tail_rows = tail_out.shape[1]
    chunks = cols * depth // half
    each = wide // cols

    def keep(relation, parts):
        @pl.when(relation // each == t)
        def _():
            at = relation % each
            for ref, start, take in parts:
                for i in range(chunks):
                    pieces[at, pl.ds(pl.multiple_of(start, take), take), i * half : (i + 1) * half] = (
                        ref[i * take : (i + 1) * take, :]
                    )

    keep(w, [(own_ref, 0, core_rows)])
    keep(w ^ 1, [(joint[0], s * span, span), (joint[1], (1 - s) * span, span)])
    lead = [(own_ref, chunks * core_rows, 0), (joint[0], chunks * span, 0)]
    for j, (outer_in, outer_swap, sum_in, sum_swap) in enumerate(fars, 1):
        keep(w ^ (2 * j + 1 - s), [(outer_in, 0, core_rows)])
        keep(w ^ (2 * j + s), [(outer_swap, 0, core_rows)])
        lead += [(sum_in, 0, 0), (sum_swap, 0, 1)]
    heads = dim // half * chunk
    pitch = -(-tail_rows // 8) * 8
    for i in range(dim // half):
        total = sum(ref[at + part * heads + i * chunk : at + part * heads + (i + 1) * chunk, :] for ref, at, part in lead)
        head_out[:, i * half : (i + 1) * half] = total * scales[0]
    total = 0.0
    for n, (ref, at, part) in enumerate(lead):
        at += heads if n < 2 else 2 * heads + part * pitch
        total = total + ref[at : at + tail_rows, :]
    tail_out[0] = total * scales[1]
    tails = split(jnp.concatenate([tail_ref[...]] + [x[0:depth, :] for x in x_refs], axis=0))
    whole = pieces[...].reshape(each * core_rows, cols * depth)
    core_out[...] = (dot3(split(whole), tails, NN) * scales[2]).reshape(each, core_rows, half)


def call(kernel, inputs, outputs, scratch=(), hbm=(), flops=0, limit=VMEM_LIMIT, traffic=None):
    vmem, far = pl.BlockSpec(memory_space=pltpu.VMEM), pl.BlockSpec(memory_space=pltpu.HBM)
    return pl.pallas_call(
        kernel,
        out_shape=tuple(jax.ShapeDtypeStruct(shape, F32) for shape in outputs),
        in_specs=[far if i in hbm else vmem for i in range(len(inputs))],
        out_specs=tuple(vmem for _ in outputs),
        scratch_shapes=[pltpu.VMEM(item, F32) if isinstance(item, tuple) else item for item in scratch],
        compiler_params=pltpu.CompilerParams(vmem_limit_bytes=limit),
        cost_estimate=pl.CostEstimate(flops=flops, bytes_accessed=4 * sum(x.size for x in inputs) if traffic is None else traffic, transcendentals=0),
    )(*inputs)


def body(head_embed, tail_embed, core_mats, labels, core_lists):
    wide, cols = lax.axis_size("wide"), lax.axis_size("tail")
    block, dim = head_embed.shape
    depth, half = tail_embed.shape
    slots = core_lists.shape[1]
    rows = block // 2
    chunk = rows // cols
    axes = ("wide", "tail", "sub")

    def move(value, k, offsets=(0, 0), flip=0, owners=False):
        steps = k if isinstance(k, tuple) else (k, k)
        pairs = []
        for w in range(wide):
            for t in range(cols):
                for s in range(2):
                    line = t ^ offsets[s]
                    if not owners or line == w // (wide // cols):
                        target = ((w ^ steps[s]) * cols + line) * 2 + (s ^ flip)
                        pairs.append(((w * cols + t) * 2 + s, target))
        return lax.ppermute(value, axes, pairs)

    core_other = move(core_mats, 0, flip=1)
    order = [wide - 1] + list(range(1, wide - 1))
    packed = call(
        functools.partial(pack_kernel, wide, cols),
        (core_lists, labels, head_embed, tail_embed, core_mats),
        [(block, half + depth)] * (wide - 1)
        + [(depth + rows + 8, half), (block + 8, depth)],
        scratch=[
            pltpu.SMEM(core_lists.shape, jnp.int32),
            pltpu.VMEM(labels.shape, jnp.int32),
            head_embed.shape,
            pltpu.SemaphoreType.DMA((4,)),
        ],
        hbm=range(5),
        limit=FULL_LIMIT,
    )
    z_out, (x_out, label_own) = packed[: wide - 1], packed[wide - 1 :]
    z_in, z_swap = {}, {}
    for k in order:
        got = []
        for j in range(max(1, cols // 2)):
            sent = z_out[k - 1] if j == 0 else z_out[k - 1][:, half:]
            got.append(move(sent, k, (2 * j, (2 * j + 1) % cols)))
        z_in[k] = got
    x_in = [move(x_out, 0, (o, o)) for o in range(1, cols)]
    tail_other = move(lax.optimization_barrier((tail_embed, core_other))[0], 0, flip=1)
    ready = lax.optimization_barrier((x_in, z_in[order[0]]))[0]
    x_other = [move(value, 0, flip=1) for value in ready]
    (query,) = call(
        query_kernel,
        (core_mats, core_other, tail_other, *x_other, tail_embed, *x_in),
        [(dim, cols * depth)],
        traffic=0,
    )
    for k in order:
        ready = z_in[k]
        z_swap[k] = [move(value, 0, flip=1) for value in ready]

    per = len(z_in[1])
    flat_in = [value for k in order for value in z_in[k]]
    flat_swap = [value for k in order for value in z_swap[k]]
    core_rows, tail_rows = dim // wide, depth // wide
    chunks = cols * depth // half
    small = dim // half * chunk + -(-tail_rows // 8) * 8
    own_shape = (chunks * core_rows + small, half)
    joint_shape = (chunks * core_rows // 2 + small, half)
    pairs = range(1, wide // 2)

    def grads(core_ref, other_ref, query_ref, head_ref, label_ref, *rest):
        x_refs, rest = rest[: cols - 1], rest[cols - 1 :]
        count = len(flat_in)
        group = lambda refs: [refs[order.index(k) * per : order.index(k) * per + per] for k in range(1, wide)]
        z_refs, swap_refs, rest = group(rest[:count]), group(rest[count : 2 * count]), rest[2 * count :]
        own_ref, joint_ref, rest = rest[0], rest[1], rest[2:]
        fars, scratch = list(zip(rest[0 : 2 * len(pairs) : 2], rest[1 : 2 * len(pairs) : 2])), rest[2 * len(pairs) :]
        grad_kernel(
            wide, cols,
            (core_ref, other_ref, query_ref, head_ref, label_ref, x_refs, z_refs, swap_refs, own_ref, joint_ref, fars)
            + tuple(scratch),
        )

    made = call(
        grads,
        (core_mats, core_other, query, head_embed, label_own, *x_in, *flat_in, *flat_swap),
        [own_shape, joint_shape] + [(chunks * core_rows, half), (2 * small, half)] * len(pairs),
        scratch=[
            (wide * block, dim), (wide * block, cols * depth), (dim, cols * depth), (cols * depth, wide * block),
        ],
        flops=6 * wide * block * dim * cols * depth * 2,
    )
    own, far = made[0], []
    for j in pairs:
        steps = (2 * j + 1, 2 * j)
        far.append([move(made[2 * j], steps, (0, 1), owners=True), move(made[2 * j + 1], steps, (0, 1))])
    joint = move(made[1], 1)
    far = [(a, move(a, 0, flip=1), b, move(b, 0, flip=1)) for a, b in far]
    joint_swap = move(joint, 0, flip=1)
    heads_total, tails_total = block * wide, depth * cols
    scales = (
        1.0 / math.sqrt(slots * tails_total),
        1.0 / math.sqrt(slots * heads_total),
        1.0 / math.sqrt(heads_total * depth),
    )
    each = wide // cols

    def finish(own_ref, *rest):
        far_s, rest = rest[: 2 * len(pairs)], rest[2 * len(pairs) :]
        joint_refs, rest = rest[:2], rest[2:]
        far_u, rest = rest[: 2 * len(pairs)], rest[2 * len(pairs) :]
        tail_ref, x_refs, rest = rest[0], rest[1:cols], rest[cols:]
        fars = [far_u[2 * i : 2 * i + 2] + far_s[2 * i : 2 * i + 2] for i in range(len(pairs))]
        finish_kernel(wide, cols, scales, tail_ref, x_refs, own_ref, joint_refs, fars, *rest)

    return call(
        finish,
        (own, *[v for g in far for v in g[2:]], joint, joint_swap, *[v for g in far for v in g[:2]], tail_embed, *x_in),
        [(chunk, dim), (1, tail_rows, half), (each, core_rows, half)],
        scratch=[(each, core_rows, cols * depth)],
        flops=6 * each * core_rows * cols * depth * half,
    )


def solution(mesh):
    in_specs = (
        P(("groups", "wide"), None),
        P(("groups", "tail"), "sub"),
        P(("groups", "wide"), None, "sub"),
        P(("groups", "wide"), None, "tail"),
        P(("groups", "tail"), None),
    )
    out_specs = (
        P(("groups", "wide", "tail", "sub"), None),
        P(("groups", "tail"), "wide", "sub"),
        P(("groups", "tail"), "wide", "sub"),
    )
    return jax.shard_map(body, mesh=mesh, in_specs=in_specs, out_specs=out_specs, check_vma=False)
```

```python
import functools
import math

import jax
import jax.numpy as jnp
from jax import lax
from jax.experimental import pallas as pl
from jax.experimental.pallas import tpu as pltpu
from jax.sharding import PartitionSpec as P


F32 = jnp.float32
VMEM_LIMIT = 48 * 1024 * 1024
FULL_LIMIT = 62 * 1024 * 1024
NN = (((1,), (0,)), ((), ()))
NT = (((1,), (1,)), ((), ()))
TN = (((0,), (0,)), ((), ()))


def split(value):
    high = value.astype(jnp.bfloat16)
    low = (value - high.astype(F32)).astype(jnp.bfloat16)
    return high, low


def dot3(left, right, dims):
    lh, ll = left
    rh, rl = right
    mul = functools.partial(lax.dot_general, dimension_numbers=dims, preferred_element_type=F32)
    free = 1 - dims[0][0][0]
    size = lh.shape[free]
    both = mul(jnp.concatenate([lh, ll], axis=free), rh)
    return both[:size] + (mul(lh, rl) + both[size:])


def window(ref, index, count):
    size = max(count, 8)
    return ref[pl.ds(pl.multiple_of(index * count // size * size, size), size), :]


def pick(value, index, count):
    if count % 8 == 0:
        return value
    per = 8 // count
    found = value[0:count]
    for i in range(1, per):
        found = jnp.where(index % per == i, value[i * count : (i + 1) * count], found)
    return found


def place():
    return lax.axis_index("wide"), lax.axis_index("tail"), lax.axis_index("sub")


def pack_kernel(wide, cols, list_hbm, label_hbm, head_hbm, tail_hbm, core_hbm, *refs):
    z_refs, (x_ref, label_own, listed, label_ref, head_ref, sems) = refs[: wide - 1], refs[wide - 1 :]
    w, t, s = place()
    block, slots, width = label_ref.shape
    chunk = block // (2 * cols)
    rows = block // 2
    depth, half = tail_hbm.shape
    starts = [pl.multiple_of((col * 2 + (s ^ part)) * chunk, chunk) for part in range(2) for col in range(cols)]
    rooms = [pl.ds(start, chunk) for start in starts]
    whole = ((list_hbm, listed), (head_hbm, head_ref), (tail_hbm, x_ref.at[0:depth]))
    sources = whole[:1] + tuple((label_hbm.at[room], label_ref.at[room]) for room in rooms) + whole[1:]
    copies = [pltpu.make_async_copy(source, target, sems.at[i]) for i, (source, target) in enumerate(sources)]
    for copy in copies:
        copy.start()
    copies[0].wait()
    count = jnp.int32(0)
    for j in range(slots):
        count = count + (listed[0, j] == w).astype(jnp.int32)
    x_ref[depth + rows :, :] = jnp.full((8, half), count.astype(F32), F32)
    label_own[block:, :] = jnp.full((8, width), count.astype(F32), F32)
    copies[-2].wait()
    for part in range(2):
        for col in range(cols):
            start = starts[part * cols + col]
            copies[1 + part * cols + col].wait()
            at = part * rows + col * chunk
            embed = head_ref[pl.ds(start, chunk), :]
            slot_labels = [label_ref[pl.ds(start, chunk), j, :] for j in range(slots)]
            for k in range(wide):
                total = jnp.zeros((chunk, width), jnp.int32)
                for j in range(slots):
                    total = total + jnp.where(listed[0, j] == (w ^ k), slot_labels[j], 0)
                total = total.astype(F32)
                if k == 0:
                    label_own[at : at + chunk, :] = total
                    lane = (at // rows) * width
                    row = depth + at % rows
                    x_ref[row : row + chunk, lane : lane + width] = total
                else:
                    z_refs[k - 1][at : at + chunk, half : half + width] = total
                    if part == 0:
                        z_refs[k - 1][at : at + chunk, 0:half] = embed[:, 0:half]
                        z_refs[k - 1][rows + at : rows + at + chunk, 0:half] = embed[:, half:]
    copies[-1].wait()


def query_kernel(core_ref, core_other, *refs):
    others, tails, out_ref = refs[: len(refs) // 2], refs[len(refs) // 2 : -1], refs[-1]
    depth = tails[0].shape[0]
    total = None
    for core, parts in ((core_ref, tails), (core_other, others)):
        tail = jnp.concatenate([ref[0:depth, :] for ref in parts], axis=0)
        value = dot3(split(core[0]), split(tail), NT)
        total = value if total is None else total + value
    out_ref[...] = total


def grad_kernel(wide, cols, refs):
    (core_ref, core_other, query_ref, head_own, label_own, x_refs, z_refs, swap_refs, own_ref, joint_ref, fars,
     heads, resid, outer, turned) = refs
    w, t, s = place()
    block, dim = head_own.shape
    width = label_own.shape[1]
    rows = block // 2
    chunk = rows // cols
    half = core_ref.shape[2]
    for i in range(2 * cols):
        part, col = divmod(i, cols)
        start = pl.multiple_of((col * 2 + (s ^ part)) * chunk, chunk)
        heads[i * chunk : (i + 1) * chunk, :] = head_own[pl.ds(start, chunk), :]
    for k in range(1, wide):
        at = k * block
        for part, ref in enumerate((z_refs[k - 1][0], swap_refs[k - 1][0])):
            heads[at + part * rows : at + part * rows + rows, 0:half] = ref[0:rows, 0:half]
            heads[at + part * rows : at + part * rows + rows, half:] = ref[rows:, 0:half]
    query = split(query_ref[...])
    head_parts = split(heads[...])
    score = dot3(head_parts, query, NN)
    prob = jax.nn.sigmoid(score)
    depth = x_refs[0].shape[0] - 8 - rows if x_refs else 0
    for o in range(cols):
        lanes = slice(o * width, (o + 1) * width)
        times = label_own[block : block + 1, :] if o == 0 else x_refs[o - 1][depth + rows : depth + rows + 1, 0:width]
        if o == 0:
            resid[0:block, lanes] = times * prob[0:block, lanes] - label_own[0:block, :]
        else:
            ref = x_refs[o - 1]
            for part in range(2):
                resid[part * rows : part * rows + rows, lanes] = (
                    times * prob[part * rows : part * rows + rows, lanes]
                    - ref[depth : depth + rows, part * width : (part + 1) * width]
                )
        for k in range(1, wide):
            first, last = (half, half + width) if o < 2 else (0, width)
            mine = z_refs[k - 1][o // 2][:, first:last]
            other = swap_refs[k - 1][o // 2]
            other = jnp.concatenate([other[rows:, first:last], other[0:rows, first:last]], axis=0)
            label = jnp.where(s == o % 2, mine, other)
            resid[k * block : (k + 1) * block, lanes] = times * prob[k * block : (k + 1) * block, lanes] - label
    resid_parts = split(resid[...])
    starts = [k * block + t * chunk for k in range(2)]
    for j in range(1, wide // 2):
        starts += [(2 * j + 1 - s) * block + part * rows + (t ^ s) * chunk for part in range(2)]
    picked = [resid[pl.ds(pl.multiple_of(start, chunk), chunk), :] for start in starts]
    head_sum = dot3(split(jnp.concatenate(picked, axis=0)), query, NT)
    outer[...] = dot3(head_parts, resid_parts, TN)
    turned[...] = resid[...].T
    tail_rows = width // wide
    pitch = max(tail_rows, 8)
    asked = [w, w ^ 1] + [s * wide + (w ^ (2 * j + 1 - s)) for j in range(1, wide // 2)]
    mixed = dot3(split(jnp.concatenate([window(turned, index, tail_rows) for index in asked], axis=0)), head_parts, NN)
    tails = dot3(split(mixed), split(core_ref[0]), NN)
    tails_other = dot3(split(mixed[2 * pitch :]), split(core_other[0]), NN)
    core_rows = dim // wide
    span = core_rows // 2

    def put_outer(ref, start, take, flip):
        piece = outer[pl.ds(pl.multiple_of(start, take), take), :]
        for i in range(cols // 2):
            first, last = piece[:, 2 * i * width : (2 * i + 1) * width], piece[:, (2 * i + 1) * width : 2 * (i + 1) * width]
            if flip:
                first, last = jnp.where(s == 0, first, last), jnp.where(s == 0, last, first)
            ref[i * take : (i + 1) * take, 0:width] = first
            ref[i * take : (i + 1) * take, width:] = last
        return cols // 2 * take

    def put_head(ref, at, item):
        for i in range(dim // half):
            ref[at : at + chunk, :] = head_sum[item * chunk : (item + 1) * chunk, i * half : (i + 1) * half]
            at += chunk
        return at

    for k, ref in enumerate((own_ref, joint_ref)):
        take = core_rows if k == 0 else span
        at = put_outer(ref, (w ^ k) * core_rows + (0 if k == 0 else s * span), take, False)
        at = put_head(ref, at, k)
        ref[at : at + tail_rows, :] = pick(tails[k * pitch : (k + 1) * pitch], w ^ k, tail_rows)
    for j, (outer_ref, sum_ref) in enumerate(fars, 1):
        target = w ^ (2 * j + 1 - s)
        put_outer(outer_ref, target * core_rows, core_rows, True)
        at = put_head(sum_ref, put_head(sum_ref, 0, 2 * j), 2 * j + 1)
        for values, first in ((tails, (j + 1) * pitch), (tails_other, (j - 1) * pitch)):
            sum_ref[at : at + tail_rows, :] = pick(values[first : first + pitch], target, tail_rows)
            at += pitch


def finish_kernel(wide, cols, scales, tail_ref, x_refs, own_ref, joint, fars, head_out, tail_out, core_out, pieces):
    w, t, s = place()
    depth, half = tail_ref.shape
    core_rows = core_out.shape[1]
    span = core_rows // 2
    chunk, dim = head_out.shape
    tail_rows = tail_out.shape[1]
    chunks = cols * depth // half
    each = wide // cols

    def keep(relation, parts):
        @pl.when(relation // each == t)
        def _():
            at = relation % each
            for ref, start, take in parts:
                for i in range(chunks):
                    pieces[at, pl.ds(pl.multiple_of(start, take), take), i * half : (i + 1) * half] = (
                        ref[i * take : (i + 1) * take, :]
                    )

    keep(w, [(own_ref, 0, core_rows)])
    keep(w ^ 1, [(joint[0], s * span, span), (joint[1], (1 - s) * span, span)])
    lead = [(own_ref, chunks * core_rows, 0), (joint[0], chunks * span, 0)]
    for j, (outer_in, outer_swap, sum_in, sum_swap) in enumerate(fars, 1):
        keep(w ^ (2 * j + 1 - s), [(outer_in, 0, core_rows)])
        keep(w ^ (2 * j + s), [(outer_swap, 0, core_rows)])
        lead += [(sum_in, 0, 0), (sum_swap, 0, 1)]
    heads = dim // half * chunk
    pitch = -(-tail_rows // 8) * 8
    for i in range(dim // half):
        total = sum(ref[at + part * heads + i * chunk : at + part * heads + (i + 1) * chunk, :] for ref, at, part in lead)
        head_out[:, i * half : (i + 1) * half] = total * scales[0]
    total = 0.0
    for n, (ref, at, part) in enumerate(lead):
        at += heads if n < 2 else 2 * heads + part * pitch
        total = total + ref[at : at + tail_rows, :]
    tail_out[0] = total * scales[1]
    tails = split(jnp.concatenate([tail_ref[...]] + [x[0:depth, :] for x in x_refs], axis=0))
    whole = pieces[...].reshape(each * core_rows, cols * depth)
    core_out[...] = (dot3(split(whole), tails, NN) * scales[2]).reshape(each, core_rows, half)


def call(kernel, inputs, outputs, scratch=(), hbm=(), flops=0, limit=VMEM_LIMIT, traffic=None):
    vmem, far = pl.BlockSpec(memory_space=pltpu.VMEM), pl.BlockSpec(memory_space=pltpu.HBM)
    return pl.pallas_call(
        kernel,
        out_shape=tuple(jax.ShapeDtypeStruct(shape, F32) for shape in outputs),
        in_specs=[far if i in hbm else vmem for i in range(len(inputs))],
        out_specs=tuple(vmem for _ in outputs),
        scratch_shapes=[pltpu.VMEM(item, F32) if isinstance(item, tuple) else item for item in scratch],
        compiler_params=pltpu.CompilerParams(vmem_limit_bytes=limit),
        cost_estimate=pl.CostEstimate(flops=flops, bytes_accessed=4 * sum(x.size for x in inputs) if traffic is None else traffic, transcendentals=0),
    )(*inputs)


def body(head_embed, tail_embed, core_mats, labels, core_lists):
    wide, cols = lax.axis_size("wide"), lax.axis_size("tail")
    block, dim = head_embed.shape
    depth, half = tail_embed.shape
    slots = core_lists.shape[1]
    rows = block // 2
    chunk = rows // cols
    axes = ("wide", "tail", "sub")

    def move(value, k, offsets=(0, 0), flip=0, owners=False):
        steps = k if isinstance(k, tuple) else (k, k)
        pairs = []
        for w in range(wide):
            for t in range(cols):
                for s in range(2):
                    line = t ^ offsets[s]
                    if not owners or line == w // (wide // cols):
                        target = ((w ^ steps[s]) * cols + line) * 2 + (s ^ flip)
                        pairs.append(((w * cols + t) * 2 + s, target))
        return lax.ppermute(value, axes, pairs)

    core_other = move(core_mats, 0, flip=1)
    order = [wide - 1] + list(range(1, wide - 1))
    packed = call(
        functools.partial(pack_kernel, wide, cols),
        (core_lists, labels, head_embed, tail_embed, core_mats),
        [(block, half + depth)] * (wide - 1)
        + [(depth + rows + 8, half), (block + 8, depth)],
        scratch=[
            pltpu.SMEM(core_lists.shape, jnp.int32),
            pltpu.VMEM(labels.shape, jnp.int32),
            head_embed.shape,
            pltpu.SemaphoreType.DMA((3 + 2 * cols,)),
        ],
        hbm=range(5),
        limit=FULL_LIMIT,
    )
    z_out, (x_out, label_own) = packed[: wide - 1], packed[wide - 1 :]
    z_in, z_swap = {}, {}
    for k in order:
        got = []
        for j in range(max(1, cols // 2)):
            sent = z_out[k - 1] if j == 0 else z_out[k - 1][:, half:]
            got.append(move(sent, k, (2 * j, (2 * j + 1) % cols)))
        z_in[k] = got
    x_in = [move(x_out, 0, (o, o)) for o in range(1, cols)]
    tail_other = move(lax.optimization_barrier((tail_embed, core_other))[0], 0, flip=1)
    ready = lax.optimization_barrier((x_in, z_in[order[0]]))[0]
    x_other = [move(value, 0, flip=1) for value in ready]
    (query,) = call(
        query_kernel,
        (core_mats, core_other, tail_other, *x_other, tail_embed, *x_in),
        [(dim, cols * depth)],
        traffic=0,
    )
    for k in order:
        ready = z_in[k]
        z_swap[k] = [move(value, 0, flip=1) for value in ready]

    per = len(z_in[1])
    flat_in = [value for k in order for value in z_in[k]]
    flat_swap = [value for k in order for value in z_swap[k]]
    core_rows, tail_rows = dim // wide, depth // wide
    chunks = cols * depth // half
    small = dim // half * chunk + -(-tail_rows // 8) * 8
    own_shape = (chunks * core_rows + small, half)
    joint_shape = (chunks * core_rows // 2 + small, half)
    pairs = range(1, wide // 2)

    def grads(core_ref, other_ref, query_ref, head_ref, label_ref, *rest):
        x_refs, rest = rest[: cols - 1], rest[cols - 1 :]
        count = len(flat_in)
        group = lambda refs: [refs[order.index(k) * per : order.index(k) * per + per] for k in range(1, wide)]
        z_refs, swap_refs, rest = group(rest[:count]), group(rest[count : 2 * count]), rest[2 * count :]
        own_ref, joint_ref, rest = rest[0], rest[1], rest[2:]
        fars, scratch = list(zip(rest[0 : 2 * len(pairs) : 2], rest[1 : 2 * len(pairs) : 2])), rest[2 * len(pairs) :]
        grad_kernel(
            wide, cols,
            (core_ref, other_ref, query_ref, head_ref, label_ref, x_refs, z_refs, swap_refs, own_ref, joint_ref, fars)
            + tuple(scratch),
        )

    made = call(
        grads,
        (core_mats, core_other, query, head_embed, label_own, *x_in, *flat_in, *flat_swap),
        [own_shape, joint_shape] + [(chunks * core_rows, half), (2 * small, half)] * len(pairs),
        scratch=[
            (wide * block, dim), (wide * block, cols * depth), (dim, cols * depth), (cols * depth, wide * block),
        ],
        flops=6 * wide * block * dim * cols * depth * 2,
    )
    own, far = made[0], []
    for j in pairs:
        steps = (2 * j + 1, 2 * j)
        far.append([move(made[2 * j], steps, (0, 1), owners=True), move(made[2 * j + 1], steps, (0, 1))])
    joint = move(made[1], 1)
    far = [(a, move(a, 0, flip=1), b, move(b, 0, flip=1)) for a, b in far]
    joint_swap = move(joint, 0, flip=1)
    heads_total, tails_total = block * wide, depth * cols
    scales = (
        1.0 / math.sqrt(slots * tails_total),
        1.0 / math.sqrt(slots * heads_total),
        1.0 / math.sqrt(heads_total * depth),
    )
    each = wide // cols

    def finish(own_ref, *rest):
        far_s, rest = rest[: 2 * len(pairs)], rest[2 * len(pairs) :]
        joint_refs, rest = rest[:2], rest[2:]
        far_u, rest = rest[: 2 * len(pairs)], rest[2 * len(pairs) :]
        tail_ref, x_refs, rest = rest[0], rest[1:cols], rest[cols:]
        fars = [far_u[2 * i : 2 * i + 2] + far_s[2 * i : 2 * i + 2] for i in range(len(pairs))]
        finish_kernel(wide, cols, scales, tail_ref, x_refs, own_ref, joint_refs, fars, *rest)

    return call(
        finish,
        (own, *[v for g in far for v in g[2:]], joint, joint_swap, *[v for g in far for v in g[:2]], tail_embed, *x_in),
        [(chunk, dim), (1, tail_rows, half), (each, core_rows, half)],
        scratch=[(each, core_rows, cols * depth)],
        flops=6 * each * core_rows * cols * depth * half,
    )


def solution(mesh):
    in_specs = (
        P(("groups", "wide"), None),
        P(("groups", "tail"), "sub"),
        P(("groups", "wide"), None, "sub"),
        P(("groups", "wide"), None, "tail"),
        P(("groups", "tail"), None),
    )
    out_specs = (
        P(("groups", "wide", "tail", "sub"), None),
        P(("groups", "tail"), "wide", "sub"),
        P(("groups", "tail"), "wide", "sub"),
    )
    return jax.shard_map(body, mesh=mesh, in_specs=in_specs, out_specs=out_specs, check_vma=False)
```

```python
import functools
import math

import jax
import jax.numpy as jnp
from jax import lax
from jax.experimental import pallas as pl
from jax.experimental.pallas import tpu as pltpu
from jax.sharding import PartitionSpec as P


F32 = jnp.float32
VMEM_LIMIT = 48 * 1024 * 1024
FULL_LIMIT = 62 * 1024 * 1024
NN = (((1,), (0,)), ((), ()))
NT = (((1,), (1,)), ((), ()))
TN = (((0,), (0,)), ((), ()))


def split(value):
    high = value.astype(jnp.bfloat16)
    low = (value - high.astype(F32)).astype(jnp.bfloat16)
    return high, low


def dot3(left, right, dims):
    lh, ll = left
    rh, rl = right
    mul = functools.partial(lax.dot_general, dimension_numbers=dims, preferred_element_type=F32)
    free = 1 - dims[0][0][0]
    size = lh.shape[free]
    both = mul(jnp.concatenate([lh, ll], axis=free), rh)
    return both[:size] + (mul(lh, rl) + both[size:])


def window(ref, index, count):
    size = max(count, 8)
    return ref[pl.ds(pl.multiple_of(index * count // size * size, size), size), :]


def pick(value, index, count):
    if count % 8 == 0:
        return value
    per = 8 // count
    found = value[0:count]
    for i in range(1, per):
        found = jnp.where(index % per == i, value[i * count : (i + 1) * count], found)
    return found


def place():
    return lax.axis_index("wide"), lax.axis_index("tail"), lax.axis_index("sub")


def pack_kernel(wide, cols, list_hbm, label_hbm, head_hbm, tail_hbm, core_hbm, *refs):
    z_refs, (x_ref, head_own, label_own, listed, label_ref, head_ref, sems) = refs[: wide - 1], refs[wide - 1 :]
    w, t, s = place()
    block, slots, width = label_ref.shape
    chunk = block // (2 * cols)
    rows = block // 2
    depth, half = tail_hbm.shape
    copies = [
        pltpu.make_async_copy(source, target, sems.at[i])
        for i, (source, target) in enumerate(
            (
                (list_hbm, listed),
                (label_hbm, label_ref),
                (head_hbm, head_ref),
                (tail_hbm, x_ref.at[0:depth]),
            )
        )
    ]
    for copy in copies:
        copy.start()
    copies[0].wait()
    count = jnp.int32(0)
    for j in range(slots):
        count = count + (listed[0, j] == w).astype(jnp.int32)
    x_ref[depth + rows :, :] = jnp.full((8, half), count.astype(F32), F32)
    label_own[block:, :] = jnp.full((8, width), count.astype(F32), F32)
    copies[1].wait()
    copies[2].wait()
    for part in range(2):
        for col in range(cols):
            start = pl.multiple_of((col * 2 + (s ^ part)) * chunk, chunk)
            at = part * rows + col * chunk
            embed = head_ref[pl.ds(start, chunk), :]
            head_own[at : at + chunk, :] = embed
            slot_labels = [label_ref[pl.ds(start, chunk), j, :] for j in range(slots)]
            for k in range(wide):
                total = jnp.zeros((chunk, width), jnp.int32)
                for j in range(slots):
                    total = total + jnp.where(listed[0, j] == (w ^ k), slot_labels[j], 0)
                total = total.astype(F32)
                if k == 0:
                    label_own[at : at + chunk, :] = total
                    lane = (at // rows) * width
                    row = depth + at % rows
                    x_ref[row : row + chunk, lane : lane + width] = total
                else:
                    z_refs[k - 1][at : at + chunk, half : half + width] = total
                    if part == 0:
                        z_refs[k - 1][at : at + chunk, 0:half] = embed[:, 0:half]
                        z_refs[k - 1][rows + at : rows + at + chunk, 0:half] = embed[:, half:]
    copies[3].wait()


def query_kernel(core_ref, core_other, *refs):
    others, tails, out_ref = refs[: len(refs) // 2], refs[len(refs) // 2 : -1], refs[-1]
    depth = tails[0].shape[0]
    total = None
    for core, parts in ((core_ref, tails), (core_other, others)):
        tail = jnp.concatenate([ref[0:depth, :] for ref in parts], axis=0)
        value = dot3(split(core[0]), split(tail), NT)
        total = value if total is None else total + value
    out_ref[...] = total


def grad_kernel(wide, cols, refs):
    (core_ref, core_other, query_ref, head_own, label_own, x_refs, z_refs, swap_refs, own_ref, joint_ref, fars,
     heads, resid, outer, turned) = refs
    w, t, s = place()
    block, dim = head_own.shape
    width = label_own.shape[1]
    rows = block // 2
    chunk = rows // cols
    half = core_ref.shape[2]
    heads[0:block, :] = head_own[...]
    for k in range(1, wide):
        at = k * block
        for part, ref in enumerate((z_refs[k - 1][0], swap_refs[k - 1][0])):
            heads[at + part * rows : at + part * rows + rows, 0:half] = ref[0:rows, 0:half]
            heads[at + part * rows : at + part * rows + rows, half:] = ref[rows:, 0:half]
    query = split(query_ref[...])
    head_parts = split(heads[...])
    score = dot3(head_parts, query, NN)
    prob = jax.nn.sigmoid(score)
    depth = x_refs[0].shape[0] - 8 - rows if x_refs else 0
    for o in range(cols):
        lanes = slice(o * width, (o + 1) * width)
        times = label_own[block : block + 1, :] if o == 0 else x_refs[o - 1][depth + rows : depth + rows + 1, 0:width]
        if o == 0:
            resid[0:block, lanes] = times * prob[0:block, lanes] - label_own[0:block, :]
        else:
            ref = x_refs[o - 1]
            for part in range(2):
                resid[part * rows : part * rows + rows, lanes] = (
                    times * prob[part * rows : part * rows + rows, lanes]
                    - ref[depth : depth + rows, part * width : (part + 1) * width]
                )
        for k in range(1, wide):
            first, last = (half, half + width) if o < 2 else (0, width)
            mine = z_refs[k - 1][o // 2][:, first:last]
            other = swap_refs[k - 1][o // 2]
            other = jnp.concatenate([other[rows:, first:last], other[0:rows, first:last]], axis=0)
            label = jnp.where(s == o % 2, mine, other)
            resid[k * block : (k + 1) * block, lanes] = times * prob[k * block : (k + 1) * block, lanes] - label
    resid_parts = split(resid[...])
    starts = [k * block + t * chunk for k in range(2)]
    for j in range(1, wide // 2):
        starts += [(2 * j + 1 - s) * block + part * rows + (t ^ s) * chunk for part in range(2)]
    picked = [resid[pl.ds(pl.multiple_of(start, chunk), chunk), :] for start in starts]
    head_sum = dot3(split(jnp.concatenate(picked, axis=0)), query, NT)
    outer[...] = dot3(head_parts, resid_parts, TN)
    turned[...] = resid[...].T
    tail_rows = width // wide
    pitch = max(tail_rows, 8)
    asked = [w, w ^ 1] + [s * wide + (w ^ (2 * j + 1 - s)) for j in range(1, wide // 2)]
    mixed = dot3(split(jnp.concatenate([window(turned, index, tail_rows) for index in asked], axis=0)), head_parts, NN)
    tails = dot3(split(mixed), split(core_ref[0]), NN)
    tails_other = dot3(split(mixed[2 * pitch :]), split(core_other[0]), NN)
    core_rows = dim // wide
    span = core_rows // 2

    def put_outer(ref, start, take, flip):
        piece = outer[pl.ds(pl.multiple_of(start, take), take), :]
        for i in range(cols // 2):
            first, last = piece[:, 2 * i * width : (2 * i + 1) * width], piece[:, (2 * i + 1) * width : 2 * (i + 1) * width]
            if flip:
                first, last = jnp.where(s == 0, first, last), jnp.where(s == 0, last, first)
            ref[i * take : (i + 1) * take, 0:width] = first
            ref[i * take : (i + 1) * take, width:] = last
        return cols // 2 * take

    def put_head(ref, at, item):
        for i in range(dim // half):
            ref[at : at + chunk, :] = head_sum[item * chunk : (item + 1) * chunk, i * half : (i + 1) * half]
            at += chunk
        return at

    for k, ref in enumerate((own_ref, joint_ref)):
        take = core_rows if k == 0 else span
        at = put_outer(ref, (w ^ k) * core_rows + (0 if k == 0 else s * span), take, False)
        at = put_head(ref, at, k)
        ref[at : at + tail_rows, :] = pick(tails[k * pitch : (k + 1) * pitch], w ^ k, tail_rows)
    for j, (outer_ref, sum_ref) in enumerate(fars, 1):
        target = w ^ (2 * j + 1 - s)
        put_outer(outer_ref, target * core_rows, core_rows, True)
        at = put_head(sum_ref, put_head(sum_ref, 0, 2 * j), 2 * j + 1)
        for values, first in ((tails, (j + 1) * pitch), (tails_other, (j - 1) * pitch)):
            sum_ref[at : at + tail_rows, :] = pick(values[first : first + pitch], target, tail_rows)
            at += pitch


def finish_kernel(wide, cols, scales, tail_ref, x_refs, own_ref, joint, fars, head_out, tail_out, core_out, pieces):
    w, t, s = place()
    depth, half = tail_ref.shape
    core_rows = core_out.shape[1]
    span = core_rows // 2
    chunk, dim = head_out.shape
    tail_rows = tail_out.shape[1]
    chunks = cols * depth // half
    each = wide // cols

    def keep(relation, parts):
        @pl.when(relation // each == t)
        def _():
            at = relation % each
            for ref, start, take in parts:
                for i in range(chunks):
                    pieces[at, pl.ds(pl.multiple_of(start, take), take), i * half : (i + 1) * half] = (
                        ref[i * take : (i + 1) * take, :]
                    )

    keep(w, [(own_ref, 0, core_rows)])
    keep(w ^ 1, [(joint[0], s * span, span), (joint[1], (1 - s) * span, span)])
    lead = [(own_ref, chunks * core_rows, 0), (joint[0], chunks * span, 0)]
    for j, (outer_in, outer_swap, sum_in, sum_swap) in enumerate(fars, 1):
        keep(w ^ (2 * j + 1 - s), [(outer_in, 0, core_rows)])
        keep(w ^ (2 * j + s), [(outer_swap, 0, core_rows)])
        lead += [(sum_in, 0, 0), (sum_swap, 0, 1)]
    heads = dim // half * chunk
    pitch = -(-tail_rows // 8) * 8
    for i in range(dim // half):
        total = sum(ref[at + part * heads + i * chunk : at + part * heads + (i + 1) * chunk, :] for ref, at, part in lead)
        head_out[:, i * half : (i + 1) * half] = total * scales[0]
    total = 0.0
    for n, (ref, at, part) in enumerate(lead):
        at += heads if n < 2 else 2 * heads + part * pitch
        total = total + ref[at : at + tail_rows, :]
    tail_out[0] = total * scales[1]
    tails = split(jnp.concatenate([tail_ref[...]] + [x[0:depth, :] for x in x_refs], axis=0))
    whole = pieces[...].reshape(each * core_rows, cols * depth)
    core_out[...] = (dot3(split(whole), tails, NN) * scales[2]).reshape(each, core_rows, half)


def call(kernel, inputs, outputs, scratch=(), hbm=(), flops=0, limit=VMEM_LIMIT, traffic=None):
    vmem, far = pl.BlockSpec(memory_space=pltpu.VMEM), pl.BlockSpec(memory_space=pltpu.HBM)
    return pl.pallas_call(
        kernel,
        out_shape=tuple(jax.ShapeDtypeStruct(shape, F32) for shape in outputs),
        in_specs=[far if i in hbm else vmem for i in range(len(inputs))],
        out_specs=tuple(vmem for _ in outputs),
        scratch_shapes=[pltpu.VMEM(item, F32) if isinstance(item, tuple) else item for item in scratch],
        compiler_params=pltpu.CompilerParams(vmem_limit_bytes=limit),
        cost_estimate=pl.CostEstimate(flops=flops, bytes_accessed=4 * sum(x.size for x in inputs) if traffic is None else traffic, transcendentals=0),
    )(*inputs)


def body(head_embed, tail_embed, core_mats, labels, core_lists):
    wide, cols = lax.axis_size("wide"), lax.axis_size("tail")
    block, dim = head_embed.shape
    depth, half = tail_embed.shape
    slots = core_lists.shape[1]
    rows = block // 2
    chunk = rows // cols
    axes = ("wide", "tail", "sub")

    def move(value, k, offsets=(0, 0), flip=0, owners=False):
        steps = k if isinstance(k, tuple) else (k, k)
        pairs = []
        for w in range(wide):
            for t in range(cols):
                for s in range(2):
                    line = t ^ offsets[s]
                    if not owners or line == w // (wide // cols):
                        target = ((w ^ steps[s]) * cols + line) * 2 + (s ^ flip)
                        pairs.append(((w * cols + t) * 2 + s, target))
        return lax.ppermute(value, axes, pairs)

    core_other = move(core_mats, 0, flip=1)
    order = [1] + list(range(wide - 1, 1, -1))
    packed = call(
        functools.partial(pack_kernel, wide, cols),
        (core_lists, labels, head_embed, tail_embed, core_mats),
        [(block, half + depth)] * (wide - 1)
        + [(depth + rows + 8, half), (block, dim), (block + 8, depth)],
        scratch=[
            pltpu.SMEM(core_lists.shape, jnp.int32),
            pltpu.VMEM(labels.shape, jnp.int32),
            head_embed.shape,
            pltpu.SemaphoreType.DMA((4,)),
        ],
        hbm=range(5),
        limit=FULL_LIMIT,
    )
    z_out, (x_out, head_own, label_own) = packed[: wide - 1], packed[wide - 1 :]
    z_in, z_swap = {}, {}
    for k in order:
        got = []
        for j in range(max(1, cols // 2)):
            sent = z_out[k - 1] if j == 0 else z_out[k - 1][:, half:]
            got.append(move(sent, k, (2 * j, (2 * j + 1) % cols)))
        z_in[k] = got
    x_in = [move(x_out, 0, (o, o)) for o in range(1, cols)]
    tail_other = move(lax.optimization_barrier((tail_embed, core_other))[0], 0, flip=1)
    ready = lax.optimization_barrier((x_in, z_in[wide - 1]))[0]
    x_other = [move(value, 0, flip=1) for value in ready]
    (query,) = call(
        query_kernel,
        (core_mats, core_other, tail_other, *x_other, tail_embed, *x_in),
        [(dim, cols * depth)],
        traffic=0,
    )
    for k in order:
        ready = z_in[k]
        z_swap[k] = [move(value, 0, flip=1) for value in ready]

    per = len(z_in[1])
    flat_in = [value for k in order for value in z_in[k]]
    flat_swap = [value for k in order for value in z_swap[k]]
    core_rows, tail_rows = dim // wide, depth // wide
    chunks = cols * depth // half
    small = dim // half * chunk + -(-tail_rows // 8) * 8
    own_shape = (chunks * core_rows + small, half)
    joint_shape = (chunks * core_rows // 2 + small, half)
    pairs = range(1, wide // 2)

    def grads(core_ref, other_ref, query_ref, head_ref, label_ref, *rest):
        x_refs, rest = rest[: cols - 1], rest[cols - 1 :]
        count = len(flat_in)
        group = lambda refs: [refs[order.index(k) * per : order.index(k) * per + per] for k in range(1, wide)]
        z_refs, swap_refs, rest = group(rest[:count]), group(rest[count : 2 * count]), rest[2 * count :]
        own_ref, joint_ref, rest = rest[0], rest[1], rest[2:]
        fars, scratch = list(zip(rest[0 : 2 * len(pairs) : 2], rest[1 : 2 * len(pairs) : 2])), rest[2 * len(pairs) :]
        grad_kernel(
            wide, cols,
            (core_ref, other_ref, query_ref, head_ref, label_ref, x_refs, z_refs, swap_refs, own_ref, joint_ref, fars)
            + tuple(scratch),
        )

    made = call(
        grads,
        (core_mats, core_other, query, head_own, label_own, *x_in, *flat_in, *flat_swap),
        [own_shape, joint_shape] + [(chunks * core_rows, half), (2 * small, half)] * len(pairs),
        scratch=[
            (wide * block, dim), (wide * block, cols * depth), (dim, cols * depth), (cols * depth, wide * block),
        ],
        flops=6 * wide * block * dim * cols * depth * 2,
    )
    own, far = made[0], []
    for j in pairs:
        steps = (2 * j + 1, 2 * j)
        far.append([move(made[2 * j], steps, (0, 1), owners=True), move(made[2 * j + 1], steps, (0, 1))])
    joint = move(made[1], 1)
    far = [(a, move(a, 0, flip=1), b, move(b, 0, flip=1)) for a, b in far]
    joint_swap = move(joint, 0, flip=1)
    heads_total, tails_total = block * wide, depth * cols
    scales = (
        1.0 / math.sqrt(slots * tails_total),
        1.0 / math.sqrt(slots * heads_total),
        1.0 / math.sqrt(heads_total * depth),
    )
    each = wide // cols

    def finish(own_ref, *rest):
        far_s, rest = rest[: 2 * len(pairs)], rest[2 * len(pairs) :]
        joint_refs, rest = rest[:2], rest[2:]
        far_u, rest = rest[: 2 * len(pairs)], rest[2 * len(pairs) :]
        tail_ref, x_refs, rest = rest[0], rest[1:cols], rest[cols:]
        fars = [far_u[2 * i : 2 * i + 2] + far_s[2 * i : 2 * i + 2] for i in range(len(pairs))]
        finish_kernel(wide, cols, scales, tail_ref, x_refs, own_ref, joint_refs, fars, *rest)

    return call(
        finish,
        (own, *[v for g in far for v in g[2:]], joint, joint_swap, *[v for g in far for v in g[:2]], tail_embed, *x_in),
        [(chunk, dim), (1, tail_rows, half), (each, core_rows, half)],
        scratch=[(each, core_rows, cols * depth)],
        flops=6 * each * core_rows * cols * depth * half,
    )


def solution(mesh):
    in_specs = (
        P(("groups", "wide"), None),
        P(("groups", "tail"), "sub"),
        P(("groups", "wide"), None, "sub"),
        P(("groups", "wide"), None, "tail"),
        P(("groups", "tail"), None),
    )
    out_specs = (
        P(("groups", "wide", "tail", "sub"), None),
        P(("groups", "tail"), "wide", "sub"),
        P(("groups", "tail"), "wide", "sub"),
    )
    return jax.shard_map(body, mesh=mesh, in_specs=in_specs, out_specs=out_specs, check_vma=False)
```
